32 devices in a mesh: grp: 2 (over x), ex: 4 (over y, core), qry: 4 (over z).
Axes of the slice: x: 2, y: 2, z: 4, core: 2. Of those that a mesh axis runs over, the one named last changes fastest.
Arguments:
- hidden: bfloat16 [8192, 14336], P(('grp', 'ex', 'qry')), parts along dimension 0, may hold values from -6 to 6
- out_grad: bfloat16 [8192, 4096], P(('grp', 'ex', 'qry')), parts along dimension 0, may hold values from -6 to 6
- proj_in: bfloat16 [32, 14336], replicated, may hold values from -0.046875 to 0.046875
- proj_out: bfloat16 [32, 4096], replicated, may hold values from -0.09375 to 0.09375
- lengths: int32 [32, 9], P(('grp', 'ex', 'qry')), parts along dimension 0, may hold values from 1 to 64, 256 in all within a row
- queries: bfloat16 [4096, 1024], P(('grp', 'qry'), 'ex'), parts along dimension 0, may hold values from -6 to 6
Outputs:
- scores: float32 [256, 2048], P(('grp', 'ex'), 'qry'), parts along dimension 0
The draws below stay inside these ranges and needn't reach their ends.
There are 2 independent parts, one for each index of `grp`. The reference program is written for one: setup_inputs(seed, part) draws one part's arguments, and reference() takes and returns one part's arrays. A program takes and returns all parts, laid end to end along the dimension named above; an argument that names none is the same for every part. Nothing has to cross between parts.
Inputs may be any that keep to these rules, and one draw needn't show every extreme that they name: `lengths`: in every row the first 8 entries are example token counts and the last the padding count; each row sums to 256 and its largest entry is 64.
All inputs are finite; a program needn't handle non-finite values.
Results may differ from the reference program's by a relative error of at most 0.0003.
Values may be sent and summed in bfloat16 or wider, within the bound.
No kernel may reach another device: no remote copies, remote signals or barrier semaphores. Data moves between devices by JAX's collectives and lax.ppermute only.
A program may use at most 128 MiB of HBM per device.

```python
import math
import jax
import jax.numpy as jnp
import numpy as np
from jax import lax

D = 4096
FF = 14336
RANK = 32
TOK_DEV = 256
EX_DEV = 8
MOST = 64
SHARDS = 16
TOKENS = 4096
EXAMPLES = 128
QUERIES = 2048


def level_of(own_key, shape, shards, smallest, top_value):
    factor_of = 1.0
    for position, parts in shards:
        draws = jax.random.uniform(jax.random.fold_in(jax.random.fold_in(own_key, 6), position), (parts,), jnp.float32, smallest / len(shards), top_value / len(shards))
        factor_of = factor_of * jnp.repeat(jnp.exp(draws), shape[position] // parts).reshape((-1,) + (1,) * (len(shape) - 1 - position))
    return factor_of


def profile(count, total, bound, slope):
    weights = [(1 << 20) // math.isqrt(grade ** slope) + 1 for grade in range(2, count + 1)]
    surplus, given = total - bound - (count - 1), [1] * (count - 1)
    while surplus > 0:
        candidates = [i for i in range(count - 1) if given[i] < bound]
        whole, budget = sum([weights[i] for i in candidates]), surplus
        for i in candidates:
            extra = min(bound - given[i], max(1, budget * weights[i] // whole), surplus)
            given[i] = given[i] + extra
            surplus = surplus - extra
    return np.array([bound] + given)


def uneven_parts(key, count, total, limit, slope):
    if count == 2:
        one = jax.random.randint(key, (), max(1, total - limit), min(limit, total - 1) + 1)
        return jnp.stack([one, total - one])
    tallies = jnp.asarray(profile(count, total, limit, slope), jnp.int32)
    couples = (count - 1) // 2
    source_of, sink = tallies[1:1 + 2 * couples:2], tallies[2:2 + 2 * couples:2]
    slack = jnp.minimum(source_of - 1, limit - sink)
    moved = jax.random.randint(jax.random.fold_in(key, 1), (couples,), 0, 1 << 20) % (slack + 1)
    tallies = tallies.at[1:1 + 2 * couples:2].set(source_of - moved).at[2:2 + 2 * couples:2].set(sink + moved)
    return tallies[jax.random.permutation(jax.random.fold_in(key, 2), count)]


def scatter_about(rng, dims, scale, limit, split=(), kind=jnp.bfloat16):
    level = level_of(rng, dims, split, -0.22, 0.18) if split else 1.0
    values = jax.random.normal(rng, dims, jnp.float32) * scale * level
    return jnp.minimum(jnp.maximum(values, -limit), limit).astype(kind)


def setup_inputs(seed: int = 0, part: int = 0) -> dict:
    keys = jax.random.split(jax.random.key(seed), 7)
    own_keys = jax.random.split(jax.random.fold_in(keys[6], part), 7)
    hidden = scatter_about(own_keys[0], (TOKENS, FF), 1.0, 6.0, ((0, 16),))
    out_grad = scatter_about(own_keys[1], (TOKENS, D), 1.0, 6.0, ((0, 16),))
    proj_in = scatter_about(keys[2], (RANK, FF), FF ** -0.5, 0.046875)
    proj_out = scatter_about(keys[3], (RANK, D), D ** -0.5, 0.09375)
    lengths = jax.vmap(lambda own: uneven_parts(own, EX_DEV + 1, TOK_DEV, MOST, 1))(jax.random.split(own_keys[4], SHARDS)).reshape((SHARDS, EX_DEV + 1)).astype(jnp.int32)
    queries = scatter_about(own_keys[5], (QUERIES, RANK * RANK), 1.0, 6.0, ((0, 4), (1, 4)))
    return {"hidden": hidden, "out_grad": out_grad, "proj_in": proj_in, "proj_out": proj_out, "lengths": lengths, "queries": queries}


def reference(hidden, out_grad, proj_in, proj_out, lengths, queries):
    width = RANK * RANK
    side_in = lax.dot_general(hidden.astype(jnp.float32), proj_in.astype(jnp.float32), (((1,), (1,)), ((), ())), preferred_element_type=jnp.float32)
    side_out = lax.dot_general(out_grad.astype(jnp.float32), proj_out.astype(jnp.float32), (((1,), (1,)), ((), ())), preferred_element_type=jnp.float32)
    outer = (side_out[:, :, None] * side_in[:, None, :]).reshape(SHARDS, TOK_DEV, width)
    counts = lengths[:, :EX_DEV]
    ends = jnp.cumsum(counts, axis=1)
    starts = ends - counts
    places = jnp.arange(TOK_DEV, dtype=jnp.int32)
    member = ((places[None, None, :] >= starts[:, :, None]) & (places[None, None, :] < ends[:, :, None])).astype(jnp.float32)
    vectors = jnp.einsum('set,stk->sek', member, outer, precision=lax.Precision.HIGHEST).reshape(EXAMPLES, width)
    fisher = jnp.dot(vectors.T, vectors, precision=lax.Precision.HIGHEST) / EXAMPLES
    damp = 0.1 * jnp.trace(fisher) / width + 1e-05
    fisher = fisher + damp * jnp.eye(width, dtype=jnp.float32)
    factor = jnp.linalg.cholesky(fisher)
    right = queries.astype(jnp.float32).T
    middle = lax.linalg.triangular_solve(factor, right, left_side=True, lower=True)
    solved = lax.linalg.triangular_solve(factor, middle, left_side=True, lower=True, transpose_a=True)
    return jnp.dot(vectors, solved, precision=lax.Precision.HIGHEST)
```

```python
import jax
import jax.numpy as jnp
from jax import lax
from jax.experimental import pallas as pl
from jax.experimental.pallas import tpu as pltpu
from jax.sharding import PartitionSpec as P

HIGHEST = lax.Precision.HIGHEST
F32 = jnp.float32
BF16 = jnp.bfloat16
NT = (((1,), (1,)), ((), ()))
NN = (((1,), (0,)), ((), ()))


def dot(a, b, dims=NN, precision=None):
    return lax.dot_general(a, b, dims, precision=precision, preferred_element_type=F32)


def split2(x):
    hi = x.astype(BF16)
    return hi, (x - hi.astype(F32)).astype(BF16)


def split3(x):
    hi = x.astype(BF16)
    rest = x - hi.astype(F32)
    mid = rest.astype(BF16)
    return hi, mid, (rest - mid.astype(F32)).astype(BF16)


def vectors_kernel(lengths, hidden, out_grad, proj_in, proj_out, vectors, side_in, side_out, stacked):
    step = pl.program_id(0)
    part_in = dot(proj_in[...], hidden[...], NT)
    part_out = dot(proj_out[...], out_grad[...], NT)

    @pl.when(step == 0)
    def _():
        side_in[...] = part_in
        side_out[...] = part_out

    @pl.when(step > 0)
    def _():
        side_in[...] += part_in
        side_out[...] += part_out

    @pl.when(step == pl.num_programs(0) - 1)
    def _():
        rank, tokens = side_in.shape
        examples = lengths.shape[1] - 1
        place = lax.broadcasted_iota(jnp.int32, (1, tokens), 1)
        outs = side_out[...]
        rows = []
        start = jnp.int32(0)
        for e in range(examples):
            end = start + lengths[0, e]
            inside = (place >= start) & (place < end)
            rows.append(jnp.where(inside, outs, 0.0))
            start = end
        masked = jnp.concatenate(rows, axis=0)
        stacked[:, :rank] = dot(masked, side_in[...], NT, HIGHEST)
        per = 128 // rank
        lane = lax.broadcasted_iota(jnp.int32, (examples, 128), 1) // rank
        for block in range(rank // per):
            total = None
            for k in range(per):
                piece = stacked[pl.ds(block * per + k, examples, stride=rank), :]
                if k:
                    piece = jnp.where(lane == k, pltpu.roll(piece, k * rank, axis=1), total)
                total = piece
            vectors[:, block * 128:(block + 1) * 128] = total


def example_vectors(hidden, out_grad, proj_in, proj_out, lengths):
    rank, features = proj_in.shape
    width_out = proj_out.shape[1]
    tokens = hidden.shape[0]
    examples = lengths.shape[1] - 1
    steps = 8
    kin, kout = features // steps, width_out // steps
    return pl.pallas_call(
        vectors_kernel,
        grid=(steps,),
        in_specs=[
            pl.BlockSpec(memory_space=pltpu.SMEM),
            pl.BlockSpec((tokens, kin), lambda i: (0, i)),
            pl.BlockSpec((tokens, kout), lambda i: (0, i)),
            pl.BlockSpec((rank, kin), lambda i: (0, i)),
            pl.BlockSpec((rank, kout), lambda i: (0, i)),
        ],
        out_specs=pl.BlockSpec((examples, rank * rank), lambda i: (0, 0)),
        out_shape=jax.ShapeDtypeStruct((examples, rank * rank), F32),
        scratch_shapes=[
            pltpu.VMEM((rank, tokens), F32),
            pltpu.VMEM((rank, tokens), F32),
            pltpu.VMEM((rank * examples, 128), F32),
        ],
        compiler_params=pltpu.CompilerParams(vmem_limit_bytes=24 * 2**20),
        cost_estimate=pl.CostEstimate(
            flops=2 * tokens * rank * (features + width_out),
            bytes_accessed=2 * (tokens + rank) * (features + width_out),
            transcendentals=0,
        ),
    )(lengths, hidden, out_grad, proj_in, proj_out)


def times(a, b):
    ah, am = split2(a)
    bh, bm = split2(b)
    left = jnp.concatenate([ah, am], axis=1)
    right = jnp.concatenate(
        [jnp.concatenate([bh, bm], axis=1), jnp.concatenate([bh, jnp.zeros_like(bm)], axis=1)], axis=0
    )
    both = dot(left, right)
    n = b.shape[1]
    return both[:, :n] + both[:, n:]


def scores_kernel(near, far, q0, q1, q2, q3, out, total, width):
    ex, qry = lax.axis_index("ex"), lax.axis_index("qry")
    block = q0.shape[1]
    n = total
    halves = (near, far)
    vec = jnp.concatenate([near[...], far[...]], axis=0)
    vh, vm, vl = split3(vec)
    gram = dot(vh, vh, NT) + ((dot(vh, vm, NT) + dot(vm, vh, NT)) + (dot(vm, vm, NT) + dot(vh, vl, NT) + dot(vl, vh, NT)))
    gram = gram / n
    row = lax.broadcasted_iota(jnp.int32, (n, n), 0)
    col = lax.broadcasted_iota(jnp.int32, (n, n), 1)
    eye = jnp.where(row == col, 1.0, 0.0).astype(F32)
    diag = gram * eye
    diag_row = jnp.sum(diag, axis=0, keepdims=True)
    diag_col = jnp.sum(diag, axis=1, keepdims=True)
    damp = 0.1 * jnp.sum(diag_row, axis=1, keepdims=True) / width + 1e-05
    root_row = lax.rsqrt(diag_row + damp)
    root_col = lax.rsqrt(diag_col + damp)
    system = (gram + damp * eye) * root_row * root_col
    size = jnp.max(jnp.sum(jnp.abs(system), axis=0, keepdims=True), axis=1, keepdims=True)
    inv_size = 1.0 / (0.51 * size)
    power = eye - system * inv_size
    series = eye + power
    power = times(power, power)
    for k in range(4):
        both = times(jnp.concatenate([series, power], axis=0), power)
        series = series + both[:n]
        power = both[n:]
    series = series + times(series, power)
    inverse = series * inv_size

    def refine(x):
        error = eye - dot(system, x, NN, HIGHEST)
        return x + times(x, error), jnp.max(jnp.abs(error))

    inverse, miss = refine(inverse)

    def again(state):
        x, _, turns = state
        x, left = refine(x)
        return x, left, turns + 1

    inverse, _, _ = lax.while_loop(
        lambda s: (s[1] > 1e-4) & (s[2] < 16), again, (inverse, miss, jnp.int32(0))
    )

    cross = None
    for k, q in enumerate((q0, q1, q2, q3)):
        start = pl.multiple_of((ex ^ k) * block, block)
        here = jnp.concatenate([h[:, pl.ds(start, block)] for h in halves], axis=0)
        hh, hm, hl = split3(here)
        qb = q[...]
        term = dot(hh, qb, NT) + dot(hm, qb, NT) + dot(hl, qb, NT)
        cross = term if cross is None else cross + term
    groups = lax.axis_size("qry")
    mine = out.shape[0]
    each = mine // groups
    weights = inverse[:mine] * root_row * root_col[:mine]
    result = dot(weights, cross, NN, HIGHEST)
    for g in range(groups):
        to = pl.multiple_of((qry ^ g) * each, each)
        out[pl.ds(to, each), :] = result[g * each:(g + 1) * each]


def swap(x, axis, bit):
    size = lax.axis_size(axis)
    return lax.ppermute(x, axis, [(i, i ^ bit) for i in range(size)])


def doubled(x, axis, bit):
    return jnp.concatenate([x, swap(x, axis, bit)], axis=0)


def body_small(hidden, out_grad, proj_in, proj_out, lengths, queries):
    width = proj_in.shape[0] * proj_in.shape[0]
    q1 = swap(queries, "ex", 1)
    q2 = swap(queries, "ex", 2)
    vectors = example_vectors(hidden, out_grad, proj_in, proj_out, lengths)
    vectors = doubled(vectors, "qry", 1)
    vectors = doubled(vectors, "qry", 2)
    q3 = swap(q2, "ex", 1)
    vectors = doubled(vectors, "ex", 2)
    far = swap(vectors, "ex", 1)
    total = 2 * vectors.shape[0]
    mine = total // lax.axis_size("ex")
    count = queries.shape[0]
    return pl.pallas_call(
        lambda *refs: scores_kernel(*refs, total=total, width=width),
        out_shape=jax.ShapeDtypeStruct((mine, count), F32),
        in_specs=[pl.BlockSpec(memory_space=pltpu.VMEM)] * 6,
        out_specs=pl.BlockSpec(memory_space=pltpu.VMEM),
        compiler_params=pltpu.CompilerParams(vmem_limit_bytes=24 * 2**20),
    )(vectors, far, queries, q1, q2, q3)


def body_large(hidden, out_grad, proj_in, proj_out, lengths, queries):
    width = proj_in.shape[0] * proj_in.shape[0]
    vectors = example_vectors(hidden, out_grad, proj_in, proj_out, lengths)
    every = lax.all_gather(vectors, ("ex", "qry"), axis=0, tiled=True)
    total = every.shape[0]
    gram = lax.dot_general(every, every, NT, precision=HIGHEST) / total
    damp = 0.1 * jnp.trace(gram) / width + 1e-05
    factor = jnp.linalg.cholesky(gram + damp * jnp.eye(total, dtype=F32))
    mine = total // lax.axis_size("ex")
    pick = jnp.eye(total, dtype=F32)
    own = lax.dynamic_slice_in_dim(pick, lax.axis_index("ex") * mine, mine, axis=1)
    middle = lax.linalg.triangular_solve(factor, own, left_side=True, lower=True)
    solved = lax.linalg.triangular_solve(factor, middle, left_side=True, lower=True, transpose_a=True)
    weighted = lax.dot_general(solved, every, (((0,), (0,)), ((), ())), precision=HIGHEST)
    features = lax.all_gather(queries, "ex", axis=1, tiled=True).astype(F32)
    return lax.dot_general(weighted, features, NT, precision=HIGHEST)


def solution(mesh):
    placed = (
        P(("grp", "ex", "qry"), None),
        P(("grp", "ex", "qry"), None),
        P(),
        P(),
        P(("grp", "ex", "qry"), None),
        P(("grp", "qry"), "ex"),
    )
    small = mesh.shape["ex"] == 4 and mesh.shape["qry"] == 4
    return jax.shard_map(
        body_small if small else body_large,
        mesh=mesh,
        in_specs=placed,
        out_specs=P(("grp", "ex"), "qry"),
        check_vma=False,
    )
```

```python
import jax
import jax.numpy as jnp
from jax import lax
from jax.experimental import pallas as pl
from jax.experimental.pallas import tpu as pltpu
from jax.sharding import PartitionSpec as P

HIGHEST = lax.Precision.HIGHEST
F32 = jnp.float32
BF16 = jnp.bfloat16
NT = (((1,), (1,)), ((), ()))
NN = (((1,), (0,)), ((), ()))


def dot(a, b, dims=NN, precision=None):
    return lax.dot_general(a, b, dims, precision=precision, preferred_element_type=F32)


def split2(x):
    hi = x.astype(BF16)
    return hi, (x - hi.astype(F32)).astype(BF16)


def split3(x):
    hi = x.astype(BF16)
    rest = x - hi.astype(F32)
    mid = rest.astype(BF16)
    return hi, mid, (rest - mid.astype(F32)).astype(BF16)


STEPS = 4


def vectors_kernel(
    lengths, hidden, out_grad, proj_in, proj_out, vectors, tokens_in, tokens_out, rows_in, rows_out, counts, stacked, sems
):
    rank, examples = proj_in.shape[0], vectors.shape[0]
    tokens = hidden.shape[0]
    count_copy = pltpu.make_async_copy(lengths, counts, sems.at[STEPS, 0])

    def copies(step):
        pairs = ((proj_out, rows_out), (out_grad, tokens_out), (proj_in, rows_in), (hidden, tokens_in))
        made = []
        for k, (source, target) in enumerate(pairs):
            size = source.shape[1] // STEPS
            part = pl.ds(pl.multiple_of(step * size, 128), size)
            made.append(pltpu.make_async_copy(source.at[:, part], target.at[:, part], sems.at[step, k]))
        return made

    for step in range(STEPS):
        for copy in copies(step):
            copy.start()
    count_copy.start()

    def project(step, sums):
        for copy in copies(step):
            copy.wait()
        new = []
        for total, weights, x in ((sums[0], rows_out, tokens_out), (sums[1], rows_in, tokens_in)):
            size = x.shape[1] // STEPS
            part = pl.ds(pl.multiple_of(step * size, 128), size)
            new.append(total + dot(weights[:, part], x[:, part], NT))
        return tuple(new)

    nothing = jnp.zeros((rank, tokens), F32)
    side_out, side_in = lax.fori_loop(0, STEPS, project, (nothing, nothing))
    count_copy.wait()
    place = lax.broadcasted_iota(jnp.int32, (1, tokens), 1)
    rows = []
    start = jnp.int32(0)
    for e in range(examples):
        end = start + counts[0, e]
        rows.append(jnp.where((place >= start) & (place < end), side_out, 0.0))
        start = end
    stacked[:, :rank] = dot(jnp.concatenate(rows, axis=0), side_in, NT, HIGHEST)
    per = 128 // rank
    lane = lax.broadcasted_iota(jnp.int32, (examples, 128), 1) // rank
    for block in range(rank // per):
        total = None
        for k in range(per):
            piece = stacked[pl.ds(block * per + k, examples, stride=rank), :]
            if k:
                piece = jnp.where(lane == k, pltpu.roll(piece, k * rank, axis=1), total)
            total = piece
        vectors[:, block * 128:(block + 1) * 128] = total


def example_vectors(hidden, out_grad, proj_in, proj_out, lengths):
    rank, features = proj_in.shape
    width_out = proj_out.shape[1]
    tokens = hidden.shape[0]
    examples = lengths.shape[1] - 1
    return pl.pallas_call(
        vectors_kernel,
        in_specs=[pl.BlockSpec(memory_space=pl.ANY)] * 5,
        out_specs=pl.BlockSpec(memory_space=pltpu.VMEM),
        out_shape=jax.ShapeDtypeStruct((examples, rank * rank), F32),
        scratch_shapes=[
            pltpu.VMEM((tokens, features), BF16),
            pltpu.VMEM((tokens, width_out), BF16),
            pltpu.VMEM((rank, features), BF16),
            pltpu.VMEM((rank, width_out), BF16),
            pltpu.SMEM(lengths.shape, jnp.int32),
            pltpu.VMEM((rank * examples, 128), F32),
            pltpu.SemaphoreType.DMA((STEPS + 1, 4)),
        ],
        compiler_params=pltpu.CompilerParams(vmem_limit_bytes=60 * 2**20),
        cost_estimate=pl.CostEstimate(
            flops=2 * tokens * rank * (features + width_out),
            bytes_accessed=2 * (tokens + rank) * (features + width_out),
            transcendentals=0,
        ),
    )(lengths, hidden, out_grad, proj_in, proj_out)


def times(a, b):
    ah, am = split2(a)
    bh, bm = split2(b)
    left = jnp.concatenate([ah, am], axis=1)
    right = jnp.concatenate(
        [jnp.concatenate([bh, bm], axis=1), jnp.concatenate([bh, jnp.zeros_like(bm)], axis=1)], axis=0
    )
    both = dot(left, right)
    n = b.shape[1]
    return both[:, :n] + both[:, n:]


def scores_kernel(*refs, width):
    *pieces, q0, q1, q2, q3, out = refs
    ex, qry = lax.axis_index("ex"), lax.axis_index("qry")
    block = q0.shape[1]
    vec = jnp.concatenate([piece[...] for piece in pieces], axis=0)
    n = vec.shape[0]
    vh, vm, vl = split3(vec)
    gram = dot(vh, vh, NT) + ((dot(vh, vm, NT) + dot(vm, vh, NT)) + (dot(vm, vm, NT) + dot(vh, vl, NT) + dot(vl, vh, NT)))
    gram = gram / n
    row = lax.broadcasted_iota(jnp.int32, (n, n), 0)
    col = lax.broadcasted_iota(jnp.int32, (n, n), 1)
    eye = jnp.where(row == col, 1.0, 0.0).astype(F32)
    diag = gram * eye
    diag_row = jnp.sum(diag, axis=0, keepdims=True)
    diag_col = jnp.sum(diag, axis=1, keepdims=True)
    damp = 0.1 * jnp.sum(diag_row, axis=1, keepdims=True) / width + 1e-05
    root_row = lax.rsqrt(diag_row + damp)
    root_col = lax.rsqrt(diag_col + damp)
    system = (gram + damp * eye) * root_row * root_col
    size = jnp.max(jnp.sum(jnp.abs(system), axis=0, keepdims=True), axis=1, keepdims=True)
    inv_size = 1.0 / (0.51 * size)
    power = eye - system * inv_size
    series = eye + power
    power = times(power, power)
    for k in range(4):
        both = times(jnp.concatenate([series, power], axis=0), power)
        series = series + both[:n]
        power = both[n:]
    series = series + times(series, power)
    inverse = series * inv_size

    def refine(x):
        error = eye - dot(system, x, NN, HIGHEST)
        return x + times(x, error), jnp.max(jnp.abs(error))

    inverse, miss = refine(inverse)

    def again(state):
        x, _, turns = state
        x, left = refine(x)
        return x, left, turns + 1

    inverse, _, _ = lax.while_loop(
        lambda s: (s[1] > 1e-4) & (s[2] < 16), again, (inverse, miss, jnp.int32(0))
    )

    cross = None
    for k, q in enumerate((q0, q1, q2, q3)):
        start = pl.multiple_of((ex ^ k) * block, block)
        here = jnp.concatenate([piece[:, pl.ds(start, block)] for piece in pieces], axis=0)
        hh, hm, hl = split3(here)
        qb = q[...]
        term = dot(hh, qb, NT) + dot(hm, qb, NT) + dot(hl, qb, NT)
        cross = term if cross is None else cross + term
    groups = lax.axis_size("qry")
    mine = out.shape[0]
    each = mine // groups
    weights = inverse[:mine] * root_row * root_col[:mine]
    result = dot(weights, cross, NN, HIGHEST)
    for g, away in enumerate((0, 2, 1, 3)):
        to = pl.multiple_of((qry ^ away) * each, each)
        out[pl.ds(to, each), :] = result[g * each:(g + 1) * each]


def swap(x, axis, bit):
    size = lax.axis_size(axis)
    return lax.ppermute(x, axis, [(i, i ^ bit) for i in range(size)])


def body_small(hidden, out_grad, proj_in, proj_out, lengths, queries):
    width = proj_in.shape[0] * proj_in.shape[0]
    both = ("ex", "qry")
    per = lax.axis_size("qry")
    q1 = swap(queries, "ex", 1)
    q2 = swap(queries, "ex", 2)
    vectors = example_vectors(hidden, out_grad, proj_in, proj_out, lengths)
    vectors, q1, q2 = lax.optimization_barrier((vectors, q1, q2))
    own = jnp.concatenate([vectors, swap(vectors, "qry", 2)], axis=0)
    here = (own, swap(own, "qry", 1), swap(own, "ex", 2), swap(own, both, 2 * per + 1))
    there = tuple(swap(piece, "ex", 1) for piece in here)
    q3 = swap(q2, "ex", 1)
    pieces = here + there
    total = sum(piece.shape[0] for piece in pieces)
    mine = total // lax.axis_size("ex")
    count = queries.shape[0]
    return pl.pallas_call(
        lambda *refs: scores_kernel(*refs, width=width),
        out_shape=jax.ShapeDtypeStruct((mine, count), F32),
        in_specs=[pl.BlockSpec(memory_space=pltpu.VMEM)] * (len(pieces) + 4),
        out_specs=pl.BlockSpec(memory_space=pltpu.VMEM),
        compiler_params=pltpu.CompilerParams(vmem_limit_bytes=24 * 2**20),
    )(*pieces, queries, q1, q2, q3)


def body_large(hidden, out_grad, proj_in, proj_out, lengths, queries):
    width = proj_in.shape[0] * proj_in.shape[0]
    vectors = example_vectors(hidden, out_grad, proj_in, proj_out, lengths)
    every = lax.all_gather(vectors, ("ex", "qry"), axis=0, tiled=True)
    total = every.shape[0]
    gram = lax.dot_general(every, every, NT, precision=HIGHEST) / total
    damp = 0.1 * jnp.trace(gram) / width + 1e-05
    factor = jnp.linalg.cholesky(gram + damp * jnp.eye(total, dtype=F32))
    mine = total // lax.axis_size("ex")
    pick = jnp.eye(total, dtype=F32)
    own = lax.dynamic_slice_in_dim(pick, lax.axis_index("ex") * mine, mine, axis=1)
    middle = lax.linalg.triangular_solve(factor, own, left_side=True, lower=True)
    solved = lax.linalg.triangular_solve(factor, middle, left_side=True, lower=True, transpose_a=True)
    weighted = lax.dot_general(solved, every, (((0,), (0,)), ((), ())), precision=HIGHEST)
    features = lax.all_gather(queries, "ex", axis=1, tiled=True).astype(F32)
    return lax.dot_general(weighted, features, NT, precision=HIGHEST)


def solution(mesh):
    placed = (
        P(("grp", "ex", "qry"), None),
        P(("grp", "ex", "qry"), None),
        P(),
        P(),
        P(("grp", "ex", "qry"), None),
        P(("grp", "qry"), "ex"),
    )
    small = mesh.shape["ex"] == 4 and mesh.shape["qry"] == 4
    return jax.shard_map(
        body_small if small else body_large,
        mesh=mesh,
        in_specs=placed,
        out_specs=P(("grp", "ex"), "qry"),
        check_vma=False,
    )
```

```python
import jax
import jax.numpy as jnp
from jax import lax
from jax.experimental import pallas as pl
from jax.experimental.pallas import tpu as pltpu
from jax.sharding import PartitionSpec as P

HIGHEST = lax.Precision.HIGHEST
F32 = jnp.float32
BF16 = jnp.bfloat16
NT = (((1,), (1,)), ((), ()))
NN = (((1,), (0,)), ((), ()))


def dot(a, b, dims=NN, precision=None):
    return lax.dot_general(a, b, dims, precision=precision, preferred_element_type=F32)


def split2(x):
    hi = x.astype(BF16)
    return hi, (x - hi.astype(F32)).astype(BF16)


def split3(x):
    hi = x.astype(BF16)
    rest = x - hi.astype(F32)
    mid = rest.astype(BF16)
    return hi, mid, (rest - mid.astype(F32)).astype(BF16)


STEPS = 4


def vectors_kernel(
    lengths, hidden, out_grad, proj_in, proj_out, vectors, tokens_in, tokens_out, rows_in, rows_out, counts, stacked, sems
):
    rank, examples = proj_in.shape[0], vectors.shape[0]
    tokens = hidden.shape[0]
    count_copy = pltpu.make_async_copy(lengths, counts, sems.at[STEPS, 0])

    def copies(step):
        pairs = ((proj_out, rows_out), (out_grad, tokens_out), (proj_in, rows_in), (hidden, tokens_in))
        made = []
        for k, (source, target) in enumerate(pairs):
            size = source.shape[1] // STEPS
            part = pl.ds(pl.multiple_of(step * size, 128), size)
            made.append(pltpu.make_async_copy(source.at[:, part], target.at[:, part], sems.at[step, k]))
        return made

    for step in range(STEPS):
        for copy in copies(step):
            copy.start()
    count_copy.start()

    def project(step, sums):
        for copy in copies(step):
            copy.wait()
        new = []
        for total, weights, x in ((sums[0], rows_out, tokens_out), (sums[1], rows_in, tokens_in)):
            size = x.shape[1] // STEPS
            part = pl.ds(pl.multiple_of(step * size, 128), size)
            new.append(total + dot(weights[:, part], x[:, part], NT))
        return tuple(new)

    nothing = jnp.zeros((rank, tokens), F32)
    side_out, side_in = lax.fori_loop(0, STEPS, project, (nothing, nothing))
    count_copy.wait()
    place = lax.broadcasted_iota(jnp.int32, (1, tokens), 1)
    rows = []
    start = jnp.int32(0)
    for e in range(examples):
        end = start + counts[0, e]
        rows.append(jnp.where((place >= start) & (place < end), side_out, 0.0))
        start = end
    stacked[:, :rank] = dot(jnp.concatenate(rows, axis=0), side_in, NT, HIGHEST)
    per = 128 // rank
    lane = lax.broadcasted_iota(jnp.int32, (examples, 128), 1) // rank
    for block in range(rank // per):
        total = None
        for k in range(per):
            piece = stacked[pl.ds(block * per + k, examples, stride=rank), :]
            if k:
                piece = jnp.where(lane == k, pltpu.roll(piece, k * rank, axis=1), total)
            total = piece
        vectors[:, block * 128:(block + 1) * 128] = total


def example_vectors(hidden, out_grad, proj_in, proj_out, lengths):
    rank, features = proj_in.shape
    width_out = proj_out.shape[1]
    tokens = hidden.shape[0]
    examples = lengths.shape[1] - 1
    return pl.pallas_call(
        vectors_kernel,
        in_specs=[pl.BlockSpec(memory_space=pl.ANY)] * 5,
        out_specs=pl.BlockSpec(memory_space=pltpu.VMEM),
        out_shape=jax.ShapeDtypeStruct((examples, rank * rank), F32),
        scratch_shapes=[
            pltpu.VMEM((tokens, features), BF16),
            pltpu.VMEM((tokens, width_out), BF16),
            pltpu.VMEM((rank, features), BF16),
            pltpu.VMEM((rank, width_out), BF16),
            pltpu.SMEM(lengths.shape, jnp.int32),
            pltpu.VMEM((rank * examples, 128), F32),
            pltpu.SemaphoreType.DMA((STEPS + 1, 4)),
        ],
        compiler_params=pltpu.CompilerParams(vmem_limit_bytes=55104 * 1024),
        cost_estimate=pl.CostEstimate(
            flops=2 * tokens * rank * (features + width_out),
            bytes_accessed=2 * (tokens + rank) * (features + width_out),
            transcendentals=0,
        ),
    )(lengths, hidden, out_grad, proj_in, proj_out)


def times(a, b):
    ah, am = split2(a)
    bh, bm = split2(b)
    left = jnp.concatenate([ah, am], axis=1)
    right = jnp.concatenate(
        [jnp.concatenate([bh, bm], axis=1), jnp.concatenate([bh, jnp.zeros_like(bm)], axis=1)], axis=0
    )
    both = dot(left, right)
    n = b.shape[1]
    return both[:, :n] + both[:, n:]


def scores_kernel(*refs, width):
    *pieces, q0, q1, q2, q3, out = refs
    ex, qry = lax.axis_index("ex"), lax.axis_index("qry")
    block = q0.shape[1]
    vec = jnp.concatenate([piece[...] for piece in pieces], axis=0)
    n = vec.shape[0]
    vh, vm, vl = split3(vec)
    gram = dot(vh, vh, NT) + ((dot(vh, vm, NT) + dot(vm, vh, NT)) + (dot(vm, vm, NT) + dot(vh, vl, NT) + dot(vl, vh, NT)))
    gram = gram / n
    row = lax.broadcasted_iota(jnp.int32, (n, n), 0)
    col = lax.broadcasted_iota(jnp.int32, (n, n), 1)
    eye = jnp.where(row == col, 1.0, 0.0).astype(F32)
    diag = gram * eye
    diag_row = jnp.sum(diag, axis=0, keepdims=True)
    diag_col = jnp.sum(diag, axis=1, keepdims=True)
    damp = 0.1 * jnp.sum(diag_row, axis=1, keepdims=True) / width + 1e-05
    root_row = lax.rsqrt(diag_row + damp)
    root_col = lax.rsqrt(diag_col + damp)
    system = (gram + damp * eye) * root_row * root_col
    size = jnp.max(jnp.sum(jnp.abs(system), axis=0, keepdims=True), axis=1, keepdims=True)
    inv_size = 1.0 / (0.51 * size)
    power = eye - system * inv_size
    series = eye + power
    power = times(power, power)
    for k in range(4):
        both = times(jnp.concatenate([series, power], axis=0), power)
        series = series + both[:n]
        power = both[n:]
    series = series + times(series, power)
    inverse = series * inv_size

    def refine(x):
        error = eye - dot(system, x, NN, HIGHEST)
        return x + times(x, error), jnp.max(jnp.abs(error))

    inverse, miss = refine(inverse)

    def again(state):
        x, _, turns = state
        x, left = refine(x)
        return x, left, turns + 1

    inverse, _, _ = lax.while_loop(
        lambda s: (s[1] > 1e-4) & (s[2] < 16), again, (inverse, miss, jnp.int32(0))
    )

    cross = None
    for k, q in enumerate((q0, q1, q2, q3)):
        start = pl.multiple_of((ex ^ k) * block, block)
        here = jnp.concatenate([piece[:, pl.ds(start, block)] for piece in pieces], axis=0)
        hh, hm, hl = split3(here)
        qb = q[...]
        term = dot(hh, qb, NT) + dot(hm, qb, NT) + dot(hl, qb, NT)
        cross = term if cross is None else cross + term
    groups = lax.axis_size("qry")
    mine = out.shape[0]
    each = mine // groups
    weights = inverse[:mine] * root_row * root_col[:mine]
    result = dot(weights, cross, NN, HIGHEST)
    for g, away in enumerate((0, 2, 1, 3)):
        to = pl.multiple_of((qry ^ away) * each, each)
        out[pl.ds(to, each), :] = result[g * each:(g + 1) * each]


def swap(x, axis, bit):
    size = lax.axis_size(axis)
    return lax.ppermute(x, axis, [(i, i ^ bit) for i in range(size)])


def body_small(hidden, out_grad, proj_in, proj_out, lengths, queries):
    width = proj_in.shape[0] * proj_in.shape[0]
    per = lax.axis_size("qry")
    core, y = per, 2 * per

    def cross(x, bits):
        return swap(x, ("ex", "qry"), bits)

    q1 = swap(queries, "ex", 1)
    q2 = swap(queries, "ex", 2)
    hidden, q1 = lax.optimization_barrier((hidden, q1))
    vectors = example_vectors(hidden, out_grad, proj_in, proj_out, lengths)
    own = jnp.concatenate([vectors, cross(vectors, 2)], axis=0)
    own, q1, q2 = lax.optimization_barrier((own, q1, q2))
    here = (own, cross(own, core + 1), cross(own, core + y), cross(own, core + y + 1))
    there = tuple(cross(piece, core) for piece in here)
    q3 = swap(q2, "ex", 1)
    pieces = (here[0], there[1], here[1], there[0], *here[2:], *there[2:])
    total = sum(piece.shape[0] for piece in pieces)
    mine = total // lax.axis_size("ex")
    count = queries.shape[0]
    return pl.pallas_call(
        lambda *refs: scores_kernel(*refs, width=width),
        out_shape=jax.ShapeDtypeStruct((mine, count), F32),
        in_specs=[pl.BlockSpec(memory_space=pltpu.VMEM)] * (len(pieces) + 4),
        out_specs=pl.BlockSpec(memory_space=pltpu.VMEM),
        compiler_params=pltpu.CompilerParams(vmem_limit_bytes=24 * 2**20),
    )(*pieces, queries, q1, q2, q3)


def body_large(hidden, out_grad, proj_in, proj_out, lengths, queries):
    width = proj_in.shape[0] * proj_in.shape[0]
    vectors = example_vectors(hidden, out_grad, proj_in, proj_out, lengths)
    every = lax.all_gather(vectors, ("ex", "qry"), axis=0, tiled=True)
    total = every.shape[0]
    gram = lax.dot_general(every, every, NT, precision=HIGHEST) / total
    damp = 0.1 * jnp.trace(gram) / width + 1e-05
    factor = jnp.linalg.cholesky(gram + damp * jnp.eye(total, dtype=F32))
    mine = total // lax.axis_size("ex")
    pick = jnp.eye(total, dtype=F32)
    own = lax.dynamic_slice_in_dim(pick, lax.axis_index("ex") * mine, mine, axis=1)
    middle = lax.linalg.triangular_solve(factor, own, left_side=True, lower=True)
    solved = lax.linalg.triangular_solve(factor, middle, left_side=True, lower=True, transpose_a=True)
    weighted = lax.dot_general(solved, every, (((0,), (0,)), ((), ())), precision=HIGHEST)
    features = lax.all_gather(queries, "ex", axis=1, tiled=True).astype(F32)
    return lax.dot_general(weighted, features, NT, precision=HIGHEST)


def solution(mesh):
    placed = (
        P(("grp", "ex", "qry"), None),
        P(("grp", "ex", "qry"), None),
        P(),
        P(),
        P(("grp", "ex", "qry"), None),
        P(("grp", "qry"), "ex"),
    )
    small = mesh.shape["ex"] == 4 and mesh.shape["qry"] == 4
    return jax.shard_map(
        body_small if small else body_large,
        mesh=mesh,
        in_specs=placed,
        out_specs=P(("grp", "ex"), "qry"),
        check_vma=False,
    )
```

```python
import jax
import jax.numpy as jnp
from jax import lax
from jax.experimental import pallas as pl
from jax.experimental.pallas import tpu as pltpu
from jax.sharding import PartitionSpec as P

HIGHEST = lax.Precision.HIGHEST
F32 = jnp.float32
BF16 = jnp.bfloat16
NT = (((1,), (1,)), ((), ()))
NN = (((1,), (0,)), ((), ()))


def dot(a, b, dims=NN, precision=None):
    return lax.dot_general(a, b, dims, precision=precision, preferred_element_type=F32)


def split2(x):
    hi = x.astype(BF16)
    return hi, (x - hi.astype(F32)).astype(BF16)


def split3(x):
    hi = x.astype(BF16)
    rest = x - hi.astype(F32)
    mid = rest.astype(BF16)
    return hi, mid, (rest - mid.astype(F32)).astype(BF16)


STEPS = 4


def vectors_kernel(
    lengths, hidden, out_grad, proj_in, proj_out, vectors, tokens_in, tokens_out, rows_in, rows_out, counts, stacked, sems
):
    rank, examples = proj_in.shape[0], vectors.shape[0]
    tokens = hidden.shape[0]
    count_copy = pltpu.make_async_copy(lengths, counts, sems.at[STEPS, 0])

    def copies(step):
        pairs = ((proj_out, rows_out), (out_grad, tokens_out), (proj_in, rows_in), (hidden, tokens_in))
        made = []
        for k, (source, target) in enumerate(pairs):
            size = source.shape[1] // STEPS
            part = pl.ds(pl.multiple_of(step * size, 128), size)
            made.append(pltpu.make_async_copy(source.at[:, part], target.at[:, part], sems.at[step, k]))
        return made

    for step in range(STEPS):
        for copy in copies(step):
            copy.start()
    count_copy.start()

    def project(step, sums):
        for copy in copies(step):
            copy.wait()
        new = []
        for total, weights, x in ((sums[0], rows_out, tokens_out), (sums[1], rows_in, tokens_in)):
            size = x.shape[1] // STEPS
            part = pl.ds(pl.multiple_of(step * size, 128), size)
            new.append(total + dot(weights[:, part], x[:, part], NT))
        return tuple(new)

    nothing = jnp.zeros((rank, tokens), F32)
    side_out, side_in = lax.fori_loop(0, STEPS, project, (nothing, nothing))
    count_copy.wait()
    place = lax.broadcasted_iota(jnp.int32, (1, tokens), 1)
    rows = []
    start = jnp.int32(0)
    for e in range(examples):
        end = start + counts[0, e]
        rows.append(jnp.where((place >= start) & (place < end), side_out, 0.0))
        start = end
    stacked[:, :rank] = dot(jnp.concatenate(rows, axis=0), side_in, NT, HIGHEST)
    per = 128 // rank
    lane = lax.broadcasted_iota(jnp.int32, (examples, 128), 1) // rank
    for block in range(rank // per):
        total = None
        for k in range(per):
            piece = stacked[pl.ds(block * per + k, examples, stride=rank), :]
            if k:
                piece = jnp.where(lane == k, pltpu.roll(piece, k * rank, axis=1), total)
            total = piece
        vectors[:, block * 128:(block + 1) * 128] = total


def example_vectors(hidden, out_grad, proj_in, proj_out, lengths):
    rank, features = proj_in.shape
    width_out = proj_out.shape[1]
    tokens = hidden.shape[0]
    examples = lengths.shape[1] - 1
    return pl.pallas_call(
        vectors_kernel,
        in_specs=[pl.BlockSpec(memory_space=pl.ANY)] * 5,
        out_specs=pl.BlockSpec(memory_space=pltpu.VMEM),
        out_shape=jax.ShapeDtypeStruct((examples, rank * rank), F32),
        scratch_shapes=[
            pltpu.VMEM((tokens, features), BF16),
            pltpu.VMEM((tokens, width_out), BF16),
            pltpu.VMEM((rank, features), BF16),
            pltpu.VMEM((rank, width_out), BF16),
            pltpu.SMEM(lengths.shape, jnp.int32),
            pltpu.VMEM((rank * examples, 128), F32),
            pltpu.SemaphoreType.DMA((STEPS + 1, 4)),
        ],
        compiler_params=pltpu.CompilerParams(vmem_limit_bytes=55104 * 1024),
        cost_estimate=pl.CostEstimate(
            flops=2 * tokens * rank * (features + width_out),
            bytes_accessed=2 * (tokens + rank) * (features + width_out),
            transcendentals=0,
        ),
    )(lengths, hidden, out_grad, proj_in, proj_out)


def product(a, b):
    ah, am = split2(a)
    bh, bm = split2(b)
    right = jnp.concatenate(
        [jnp.concatenate([bh, bm], axis=1), jnp.concatenate([bh, jnp.zeros_like(bm)], axis=1)], axis=0
    )
    both = dot(jnp.concatenate([ah, am], axis=1), right)
    n = b.shape[1]
    return both[:, :n] + both[:, n:]


def product6(a, b):
    ah, am, al = split3(a)
    bh, bm, bl = split3(b)
    top = jnp.concatenate([bh, bm], axis=1)
    both = dot(jnp.concatenate([ah, am], axis=1), jnp.concatenate([top, top], axis=0))
    small = dot(jnp.concatenate([al, ah], axis=1), jnp.concatenate([bh, bl], axis=0))
    n = b.shape[1]
    return both[:, :n] + (both[:, n:] + small)


def scores_kernel(*refs, width):
    *pieces, q0, q1, q2, q3, out = refs
    ex, qry = lax.axis_index("ex"), lax.axis_index("qry")
    block = q0.shape[1]
    columns = []
    for k in range(4):
        part = pl.ds(pl.multiple_of((ex ^ k) * block, block), block)
        columns.append(jnp.concatenate([piece[:, part] for piece in pieces], axis=0))
    vec = jnp.concatenate(columns, axis=1)
    n = vec.shape[0]
    vh, vm, vl = split3(vec)
    large = jnp.concatenate([vh, vm], axis=0)
    quads = dot(large, large, NT)
    tail = dot(vh, vl, NT)
    gram = quads[:n, :n] + ((quads[:n, n:] + quads[n:, :n]) + (quads[n:, n:] + (tail + tail.T)))
    gram = gram / n
    row = lax.broadcasted_iota(jnp.int32, (n, n), 0)
    col = lax.broadcasted_iota(jnp.int32, (n, n), 1)
    eye = jnp.where(row == col, 1.0, 0.0).astype(F32)
    diag = gram * eye
    diag_row = jnp.sum(diag, axis=0, keepdims=True)
    diag_col = jnp.sum(diag, axis=1, keepdims=True)
    damp = 0.1 * jnp.sum(diag_row, axis=1, keepdims=True) / width + 1e-05
    root_row = lax.rsqrt(diag_row + damp)
    root_col = lax.rsqrt(diag_col + damp)
    system = (gram + damp * eye) * root_row * root_col
    square = product(system, system)
    size = jnp.max(jnp.sum(jnp.abs(square), axis=0, keepdims=True), axis=1, keepdims=True)
    scale = (1.0 / 0.51) * lax.rsqrt(size)
    scaled = system * scale
    power = (eye - 2.0 * scaled) + square * (scale * scale)
    series = 2.0 * eye - scaled
    for _ in range(3):
        both = product(jnp.concatenate([series, power], axis=0), power)
        series = series + both[:n]
        power = both[n:]
    series = (series + product(series, power)) * scale

    wanted = jnp.concatenate([q[...] for q in (q0, q1, q2, q3)], axis=1)
    crossed = dot(jnp.concatenate([vh, vm, vl], axis=0), wanted, NT)
    cross = crossed[:n] + (crossed[n:2 * n] + crossed[2 * n:])
    mine = out.shape[0]
    groups = lax.axis_size("qry")
    each = mine // groups

    def refine(x):
        error = eye - product6(system, x)
        return x + product(x, error), jnp.sum(error * error)

    def store(x):
        weights = x[:mine] * root_row * root_col[:mine]
        result = dot(weights, cross, NN, HIGHEST)
        for g, away in enumerate((0, 2, 1, 3)):
            to = pl.multiple_of((qry ^ away) * each, each)
            out[pl.ds(to, each), :] = result[g * each:(g + 1) * each]

    inverse, miss = refine(series)
    store(inverse)

    @pl.when(miss > 1e-6)
    def _():
        def again(state):
            x, _, turns = state
            x, left = refine(x)
            return x, left, turns + 1

        store(lax.while_loop(lambda s: (s[1] > 1e-6) & (s[2] < 16), again, (inverse, miss, jnp.int32(0)))[0])


def swap(x, axis, bit):
    size = lax.axis_size(axis)
    return lax.ppermute(x, axis, [(i, i ^ bit) for i in range(size)])


def body_small(hidden, out_grad, proj_in, proj_out, lengths, queries):
    width = proj_in.shape[0] * proj_in.shape[0]
    per = lax.axis_size("qry")
    core, y = per, 2 * per

    def cross(x, bits):
        return swap(x, ("ex", "qry"), bits)

    q1 = swap(queries, "ex", 1)
    q2 = swap(queries, "ex", 2)
    hidden, q1 = lax.optimization_barrier((hidden, q1))
    vectors = example_vectors(hidden, out_grad, proj_in, proj_out, lengths)
    own = jnp.concatenate([vectors, cross(vectors, 2)], axis=0)
    own, q1, q2 = lax.optimization_barrier((own, q1, q2))
    here = (own, cross(own, core + 1), cross(own, core + y), cross(own, core + y + 1))
    there = tuple(cross(piece, core) for piece in here)
    q3 = swap(q2, "ex", 1)
    pieces = (here[0], there[1], here[1], there[0], *here[2:], *there[2:])
    total = sum(piece.shape[0] for piece in pieces)
    mine = total // lax.axis_size("ex")
    count = queries.shape[0]
    return pl.pallas_call(
        lambda *refs: scores_kernel(*refs, width=width),
        out_shape=jax.ShapeDtypeStruct((mine, count), F32),
        in_specs=[pl.BlockSpec(memory_space=pltpu.VMEM)] * (len(pieces) + 4),
        out_specs=pl.BlockSpec(memory_space=pltpu.VMEM),
        compiler_params=pltpu.CompilerParams(vmem_limit_bytes=24 * 2**20),
    )(*pieces, queries, q1, q2, q3)


def body_large(hidden, out_grad, proj_in, proj_out, lengths, queries):
    width = proj_in.shape[0] * proj_in.shape[0]
    vectors = example_vectors(hidden, out_grad, proj_in, proj_out, lengths)
    every = lax.all_gather(vectors, ("ex", "qry"), axis=0, tiled=True)
    total = every.shape[0]
    gram = lax.dot_general(every, every, NT, precision=HIGHEST) / total
    damp = 0.1 * jnp.trace(gram) / width + 1e-05
    factor = jnp.linalg.cholesky(gram + damp * jnp.eye(total, dtype=F32))
    mine = total // lax.axis_size("ex")
    pick = jnp.eye(total, dtype=F32)
    own = lax.dynamic_slice_in_dim(pick, lax.axis_index("ex") * mine, mine, axis=1)
    middle = lax.linalg.triangular_solve(factor, own, left_side=True, lower=True)
    solved = lax.linalg.triangular_solve(factor, middle, left_side=True, lower=True, transpose_a=True)
    weighted = lax.dot_general(solved, every, (((0,), (0,)), ((), ())), precision=HIGHEST)
    features = lax.all_gather(queries, "ex", axis=1, tiled=True).astype(F32)
    return lax.dot_general(weighted, features, NT, precision=HIGHEST)


def solution(mesh):
    placed = (
        P(("grp", "ex", "qry"), None),
        P(("grp", "ex", "qry"), None),
        P(),
        P(),
        P(("grp", "ex", "qry"), None),
        P(("grp", "qry"), "ex"),
    )
    small = mesh.shape["ex"] == 4 and mesh.shape["qry"] == 4
    return jax.shard_map(
        body_small if small else body_large,
        mesh=mesh,
        in_specs=placed,
        out_specs=P(("grp", "ex"), "qry"),
        check_vma=False,
    )
```

```python
import jax
import jax.numpy as jnp
from jax import lax
from jax.experimental import pallas as pl
from jax.experimental.pallas import tpu as pltpu
from jax.sharding import PartitionSpec as P

HIGHEST = lax.Precision.HIGHEST
F32 = jnp.float32
BF16 = jnp.bfloat16
NT = (((1,), (1,)), ((), ()))
NN = (((1,), (0,)), ((), ()))


def dot(a, b, dims=NN, precision=None):
    return lax.dot_general(a, b, dims, precision=precision, preferred_element_type=F32)


def split2(x):
    hi = x.astype(BF16)
    return hi, (x - hi.astype(F32)).astype(BF16)


def split3(x):
    hi = x.astype(BF16)
    rest = x - hi.astype(F32)
    mid = rest.astype(BF16)
    return hi, mid, (rest - mid.astype(F32)).astype(BF16)


STEPS = 4


def vectors_kernel(
    lengths, hidden, out_grad, proj_in, proj_out, vectors, tokens_in, tokens_out, rows_in, rows_out, counts, stacked, sems
):
    rank, examples = proj_in.shape[0], vectors.shape[0]
    tokens = hidden.shape[0]
    count_copy = pltpu.make_async_copy(lengths, counts, sems.at[STEPS, 0])

    def copies(step):
        pairs = ((proj_out, rows_out), (out_grad, tokens_out), (proj_in, rows_in), (hidden, tokens_in))
        made = []
        for k, (source, target) in enumerate(pairs):
            size = source.shape[1] // STEPS
            part = pl.ds(pl.multiple_of(step * size, 128), size)
            made.append(pltpu.make_async_copy(source.at[:, part], target.at[:, part], sems.at[step, k]))
        return made

    for step in range(STEPS):
        for copy in copies(step):
            copy.start()
    count_copy.start()

    def project(step, sums):
        for copy in copies(step):
            copy.wait()
        new = []
        for total, weights, x in ((sums[0], rows_out, tokens_out), (sums[1], rows_in, tokens_in)):
            size = x.shape[1] // STEPS
            part = pl.ds(pl.multiple_of(step * size, 128), size)
            new.append(total + dot(weights[:, part], x[:, part], NT))
        return tuple(new)

    nothing = jnp.zeros((rank, tokens), F32)
    side_out, side_in = lax.fori_loop(0, STEPS, project, (nothing, nothing))
    count_copy.wait()
    place = lax.broadcasted_iota(jnp.int32, (1, tokens), 1)
    rows = []
    start = jnp.int32(0)
    for e in range(examples):
        end = start + counts[0, e]
        rows.append(jnp.where((place >= start) & (place < end), side_out, 0.0))
        start = end
    stacked[:, :rank] = dot(jnp.concatenate(rows, axis=0), side_in, NT, HIGHEST)
    per = 128 // rank
    lane = lax.broadcasted_iota(jnp.int32, (examples, 128), 1) // rank
    for block in range(rank // per):
        total = None
        for k in range(per):
            piece = stacked[pl.ds(block * per + k, examples, stride=rank), :]
            if k:
                piece = jnp.where(lane == k, pltpu.roll(piece, k * rank, axis=1), total)
            total = piece
        vectors[:, block * 128:(block + 1) * 128] = total


def example_vectors(hidden, out_grad, proj_in, proj_out, lengths):
    rank, features = proj_in.shape
    width_out = proj_out.shape[1]
    tokens = hidden.shape[0]
    examples = lengths.shape[1] - 1
    operands = (lengths, hidden, out_grad, proj_in, proj_out)
    return pl.pallas_call(
        vectors_kernel,
        in_specs=[pl.BlockSpec(memory_space=pltpu.HBM)] * 5,
        out_specs=pl.BlockSpec(memory_space=pltpu.VMEM),
        out_shape=jax.ShapeDtypeStruct((examples, rank * rank), F32),
        scratch_shapes=[
            pltpu.VMEM((tokens, features), BF16),
            pltpu.VMEM((tokens, width_out), BF16),
            pltpu.VMEM((rank, features), BF16),
            pltpu.VMEM((rank, width_out), BF16),
            pltpu.SMEM(lengths.shape, jnp.int32),
            pltpu.VMEM((rank * examples, 128), F32),
            pltpu.SemaphoreType.DMA((STEPS + 1, 4)),
        ],
        compiler_params=pltpu.CompilerParams(vmem_limit_bytes=24 * 2**20),
        cost_estimate=pl.CostEstimate(
            flops=2 * tokens * rank * (features + width_out),
            bytes_accessed=2 * (tokens + rank) * (features + width_out),
            transcendentals=0,
        ),
    )(*(pltpu.with_memory_space_constraint(x, pltpu.HBM) for x in operands))


def product(a, b):
    ah, am = split2(a)
    bh, bm = split2(b)
    right = jnp.concatenate(
        [jnp.concatenate([bh, bm], axis=1), jnp.concatenate([bh, jnp.zeros_like(bm)], axis=1)], axis=0
    )
    both = dot(jnp.concatenate([ah, am], axis=1), right)
    n = b.shape[1]
    return both[:, :n] + both[:, n:]


def product6(a, b):
    ah, am, al = split3(a)
    bh, bm, bl = split3(b)
    top = jnp.concatenate([bh, bm], axis=1)
    both = dot(jnp.concatenate([ah, am], axis=1), jnp.concatenate([top, top], axis=0))
    small = dot(jnp.concatenate([al, ah], axis=1), jnp.concatenate([bh, bl], axis=0))
    n = b.shape[1]
    return both[:, :n] + (both[:, n:] + small)


def scores_kernel(*refs, width, rows):
    *pieces, q0, q1, q2, q3, out = refs
    ex, qry = lax.axis_index("ex"), lax.axis_index("qry")
    block = q0.shape[1]
    mine = out.shape[0]
    groups = lax.axis_size("qry")
    each = mine // groups
    columns = []
    for k in range(4):
        part = pl.ds(pl.multiple_of((ex ^ k) * block, block), block)
        columns.append(jnp.concatenate([pieces[p][half * each:(half + 1) * each, part] for _, p, half in rows], axis=0))
    vec = jnp.concatenate(columns, axis=1)
    n = vec.shape[0]
    vh, vm, vl = split3(vec)
    large = jnp.concatenate([vh, vm], axis=0)
    quads = dot(large, large, NT)
    tail = dot(vh, vl, NT)
    gram = quads[:n, :n] + ((quads[:n, n:] + quads[n:, :n]) + (quads[n:, n:] + (tail + tail.T)))
    gram = gram / n
    row = lax.broadcasted_iota(jnp.int32, (n, n), 0)
    col = lax.broadcasted_iota(jnp.int32, (n, n), 1)
    eye = jnp.where(row == col, 1.0, 0.0).astype(F32)
    diag = gram * eye
    diag_row = jnp.sum(diag, axis=0, keepdims=True)
    diag_col = jnp.sum(diag, axis=1, keepdims=True)
    damp = 0.1 * jnp.sum(diag_row, axis=1, keepdims=True) / width + 1e-05
    root_row = lax.rsqrt(diag_row + damp)
    root_col = lax.rsqrt(diag_col + damp)
    system = (gram + damp * eye) * root_row * root_col
    square = product(system, system)
    size = jnp.max(jnp.sum(jnp.abs(square), axis=0, keepdims=True), axis=1, keepdims=True)
    scale = (1.0 / 0.51) * lax.rsqrt(size)
    scaled = system * scale
    power = (eye - 2.0 * scaled) + square * (scale * scale)
    series = 2.0 * eye - scaled
    for _ in range(3):
        both = product(jnp.concatenate([series, power], axis=0), power)
        series = series + both[:n]
        power = both[n:]
    series = (series + product(series, power)) * scale

    wanted = jnp.concatenate([q[...] for q in (q0, q1, q2, q3)], axis=1)
    crossed = dot(jnp.concatenate([vh, vm, vl], axis=0), wanted, NT)
    cross = crossed[:n] + (crossed[n:2 * n] + crossed[2 * n:])

    def refine(x):
        error = eye - product6(system, x)
        return x + product(x, error), jnp.sum(error * error)

    def store(x):
        weights = x[:mine] * root_row * root_col[:mine]
        result = dot(weights, cross, NN, HIGHEST)
        for away in range(groups):
            to = pl.multiple_of((qry ^ away) * each, each)
            out[pl.ds(to, each), :] = result[away * each:(away + 1) * each]

    inverse, miss = refine(series)
    store(inverse)

    @pl.when(miss > 1e-6)
    def _():
        def again(state):
            x, _, turns = state
            x, left = refine(x)
            return x, left, turns + 1

        store(lax.while_loop(lambda s: (s[1] > 1e-6) & (s[2] < 16), again, (inverse, miss, jnp.int32(0)))[0])


def swap(x, axis, bit):
    size = lax.axis_size(axis)
    return lax.ppermute(x, axis, [(i, i ^ bit) for i in range(size)])


def body_small(hidden, out_grad, proj_in, proj_out, lengths, queries):
    width = proj_in.shape[0] * proj_in.shape[0]
    examples = lengths.shape[1] - 1
    per = lax.axis_size("qry")
    core, y = per, 2 * per

    def cross(x, bits):
        return swap(x, ("ex", "qry"), bits)

    q1 = swap(queries, "ex", 1)
    q2 = swap(queries, "ex", 2)
    vectors = example_vectors(hidden, out_grad, proj_in, proj_out, lengths)
    first = core + 2
    own = jnp.concatenate([vectors, cross(vectors, first)], axis=0)
    own, q2 = lax.optimization_barrier((own, q2))
    pieces = {0: own}
    for bits in (core + y, core + 1, core + y + 1):
        pieces[bits] = cross(own, bits)
    for bits in tuple(pieces):
        pieces[bits ^ core] = cross(pieces[bits], core)
    q3 = swap(q2, "ex", 1)
    rows = sorted((bits ^ (first * half), k, half) for k, bits in enumerate(pieces) for half in range(2))
    mine = per * examples
    count = queries.shape[0]
    return pl.pallas_call(
        lambda *refs: scores_kernel(*refs, width=width, rows=rows),
        out_shape=jax.ShapeDtypeStruct((mine, count), F32),
        in_specs=[pl.BlockSpec(memory_space=pltpu.VMEM)] * (len(pieces) + 4),
        out_specs=pl.BlockSpec(memory_space=pltpu.VMEM),
        compiler_params=pltpu.CompilerParams(vmem_limit_bytes=24 * 2**20),
    )(*pieces.values(), queries, q1, q2, q3)


def body_large(hidden, out_grad, proj_in, proj_out, lengths, queries):
    width = proj_in.shape[0] * proj_in.shape[0]
    vectors = example_vectors(hidden, out_grad, proj_in, proj_out, lengths)
    every = lax.all_gather(vectors, ("ex", "qry"), axis=0, tiled=True)
    total = every.shape[0]
    gram = lax.dot_general(every, every, NT, precision=HIGHEST) / total
    damp = 0.1 * jnp.trace(gram) / width + 1e-05
    factor = jnp.linalg.cholesky(gram + damp * jnp.eye(total, dtype=F32))
    mine = total // lax.axis_size("ex")
    pick = jnp.eye(total, dtype=F32)
    own = lax.dynamic_slice_in_dim(pick, lax.axis_index("ex") * mine, mine, axis=1)
    middle = lax.linalg.triangular_solve(factor, own, left_side=True, lower=True)
    solved = lax.linalg.triangular_solve(factor, middle, left_side=True, lower=True, transpose_a=True)
    weighted = lax.dot_general(solved, every, (((0,), (0,)), ((), ())), precision=HIGHEST)
    features = lax.all_gather(queries, "ex", axis=1, tiled=True).astype(F32)
    return lax.dot_general(weighted, features, NT, precision=HIGHEST)


def solution(mesh):
    placed = (
        P(("grp", "ex", "qry"), None),
        P(("grp", "ex", "qry"), None),
        P(),
        P(),
        P(("grp", "ex", "qry"), None),
        P(("grp", "qry"), "ex"),
    )
    small = mesh.shape["ex"] == 4 and mesh.shape["qry"] == 4
    return jax.shard_map(
        body_small if small else body_large,
        mesh=mesh,
        in_specs=placed,
        out_specs=P(("grp", "ex"), "qry"),
        check_vma=False,
    )
```

```python
import jax
import jax.numpy as jnp
from jax import lax
from jax.experimental import pallas as pl
from jax.experimental.pallas import tpu as pltpu
from jax.sharding import PartitionSpec as P

HIGHEST = lax.Precision.HIGHEST
F32 = jnp.float32
BF16 = jnp.bfloat16
NT = (((1,), (1,)), ((), ()))
NN = (((1,), (0,)), ((), ()))


def dot(a, b, dims=NN, precision=None):
    return lax.dot_general(a, b, dims, precision=precision, preferred_element_type=F32)


def split2(x):
    hi = x.astype(BF16)
    return hi, (x - hi.astype(F32)).astype(BF16)


def split3(x):
    hi = x.astype(BF16)
    rest = x - hi.astype(F32)
    mid = rest.astype(BF16)
    return hi, mid, (rest - mid.astype(F32)).astype(BF16)


STEPS = 4


def vectors_kernel(
    lengths, hidden, out_grad, proj_in, proj_out, vectors, tokens_in, tokens_out, rows_in, rows_out, counts, stacked, sems
):
    rank, examples = proj_in.shape[0], vectors.shape[0]
    tokens = hidden.shape[0]
    count_copy = pltpu.make_async_copy(lengths, counts, sems.at[STEPS, 0])

    def copies(step):
        pairs = ((proj_out, rows_out), (out_grad, tokens_out), (proj_in, rows_in), (hidden, tokens_in))
        made = []
        for k, (source, target) in enumerate(pairs):
            size = source.shape[1] // STEPS
            part = pl.ds(pl.multiple_of(step * size, 128), size)
            made.append(pltpu.make_async_copy(source.at[:, part], target.at[:, part], sems.at[step, k]))
        return made

    for step in range(STEPS):
        for copy in copies(step):
            copy.start()
    count_copy.start()

    def project(step, sums):
        for copy in copies(step):
            copy.wait()
        new = []
        for total, weights, x in ((sums[0], rows_out, tokens_out), (sums[1], rows_in, tokens_in)):
            size = x.shape[1] // STEPS
            part = pl.ds(pl.multiple_of(step * size, 128), size)
            new.append(total + dot(weights[:, part], x[:, part], NT))
        return tuple(new)

    nothing = jnp.zeros((rank, tokens), F32)
    side_out, side_in = lax.fori_loop(0, STEPS, project, (nothing, nothing))
    count_copy.wait()
    place = lax.broadcasted_iota(jnp.int32, (1, tokens), 1)
    rows = []
    start = jnp.int32(0)
    for e in range(examples):
        end = start + counts[0, e]
        rows.append(jnp.where((place >= start) & (place < end), side_out, 0.0))
        start = end
    stacked[:, :rank] = dot(jnp.concatenate(rows, axis=0), side_in, NT, HIGHEST)
    per = 128 // rank
    lane = lax.broadcasted_iota(jnp.int32, (examples, 128), 1) // rank
    for block in range(rank // per):
        total = None
        for k in range(per):
            piece = stacked[pl.ds(block * per + k, examples, stride=rank), :]
            if k:
                piece = jnp.where(lane == k, pltpu.roll(piece, k * rank, axis=1), total)
            total = piece
        vectors[:, block * 128:(block + 1) * 128] = total


def example_vectors(hidden, out_grad, proj_in, proj_out, lengths):
    rank, features = proj_in.shape
    width_out = proj_out.shape[1]
    tokens = hidden.shape[0]
    examples = lengths.shape[1] - 1
    operands = (lengths, hidden, out_grad, proj_in, proj_out)
    return pl.pallas_call(
        vectors_kernel,
        in_specs=[pl.BlockSpec(memory_space=pltpu.HBM)] * 5,
        out_specs=pl.BlockSpec(memory_space=pltpu.VMEM),
        out_shape=jax.ShapeDtypeStruct((examples, rank * rank), F32),
        scratch_shapes=[
            pltpu.VMEM((tokens, features), BF16),
            pltpu.VMEM((tokens, width_out), BF16),
            pltpu.VMEM((rank, features), BF16),
            pltpu.VMEM((rank, width_out), BF16),
            pltpu.SMEM(lengths.shape, jnp.int32),
            pltpu.VMEM((rank * examples, 128), F32),
            pltpu.SemaphoreType.DMA((STEPS + 1, 4)),
        ],
        compiler_params=pltpu.CompilerParams(vmem_limit_bytes=24 * 2**20),
        cost_estimate=pl.CostEstimate(
            flops=2 * tokens * rank * (features + width_out),
            bytes_accessed=2 * (tokens + rank) * (features + width_out),
            transcendentals=0,
        ),
    )(*(pltpu.with_memory_space_constraint(x, pltpu.HBM) for x in operands))


def product(a, b):
    ah, am = split2(a)
    bh, bm = split2(b)
    right = jnp.concatenate(
        [jnp.concatenate([bh, bm], axis=1), jnp.concatenate([bh, jnp.zeros_like(bm)], axis=1)], axis=0
    )
    both = dot(jnp.concatenate([ah, am], axis=1), right)
    n = b.shape[1]
    return both[:, :n] + both[:, n:]


def product6(a, b):
    ah, am, al = split3(a)
    bh, bm, bl = split3(b)
    top = jnp.concatenate([bh, bm], axis=1)
    both = dot(jnp.concatenate([ah, am], axis=1), jnp.concatenate([top, top], axis=0))
    small = dot(jnp.concatenate([al, ah], axis=1), jnp.concatenate([bh, bl], axis=0))
    n = b.shape[1]
    return both[:, :n] + (both[:, n:] + small)


def scores_kernel(*refs, width, rows):
    *pieces, q0, q1, q2, q3, out = refs
    ex, qry = lax.axis_index("ex"), lax.axis_index("qry")
    block = q0.shape[1]
    mine = out.shape[0]
    groups = lax.axis_size("qry")
    each = mine // groups
    columns = []
    for k in range(4):
        part = pl.ds(pl.multiple_of((ex ^ k) * block, block), block)
        columns.append(jnp.concatenate([pieces[p][half * each:(half + 1) * each, part] for _, p, half in rows], axis=0))
    vec = jnp.concatenate(columns, axis=1)
    n = vec.shape[0]
    vh, vm, vl = split3(vec)
    large = jnp.concatenate([vh, vm], axis=0)
    quads = dot(large, large, NT)
    tail = dot(vh, vl, NT)
    gram = quads[:n, :n] + ((quads[:n, n:] + quads[n:, :n]) + (quads[n:, n:] + (tail + tail.T)))
    gram = gram / n
    row = lax.broadcasted_iota(jnp.int32, (n, n), 0)
    col = lax.broadcasted_iota(jnp.int32, (n, n), 1)
    eye = jnp.where(row == col, 1.0, 0.0).astype(F32)
    diag_col = jnp.sum(vec * vec, axis=1, keepdims=True) / n
    diag_row = jnp.sum(eye * diag_col, axis=0, keepdims=True)
    damp = 0.1 * jnp.sum(diag_col, axis=0, keepdims=True) / width + 1e-05
    root_row = lax.rsqrt(diag_row + damp)
    root_col = lax.rsqrt(diag_col + damp)
    system = (gram + damp * eye) * root_row * root_col
    square = product(system, system)
    size = jnp.max(jnp.sum(jnp.abs(square), axis=0, keepdims=True), axis=1, keepdims=True)
    scale = (1.0 / 0.51) * lax.rsqrt(size)
    scaled = system * scale
    power = (eye - 2.0 * scaled) + square * (scale * scale)
    series = 2.0 * eye - scaled
    for _ in range(3):
        both = product(jnp.concatenate([series, power], axis=0), power)
        series = series + both[:n]
        power = both[n:]
    series = (series + product(series, power)) * scale

    wanted = jnp.concatenate([q[...] for q in (q0, q1, q2, q3)], axis=1)
    crossed = dot(jnp.concatenate([vh, vm, vl], axis=0), wanted, NT)
    cross = crossed[:n] + (crossed[n:2 * n] + crossed[2 * n:])

    def refine(x):
        error = eye - product6(system, x)
        return x + product(x, error), jnp.sum(error * error)

    def store(x):
        weights = x[:mine] * root_row * root_col[:mine]
        result = dot(weights, cross, NN, HIGHEST)
        for away in range(groups):
            to = pl.multiple_of((qry ^ away) * each, each)
            out[pl.ds(to, each), :] = result[away * each:(away + 1) * each]

    inverse, miss = refine(series)
    store(inverse)

    @pl.when(miss > 1e-6)
    def _():
        def again(state):
            x, _, turns = state
            x, left = refine(x)
            return x, left, turns + 1

        store(lax.while_loop(lambda s: (s[1] > 1e-6) & (s[2] < 16), again, (inverse, miss, jnp.int32(0)))[0])


def swap(x, axis, bit):
    size = lax.axis_size(axis)
    return lax.ppermute(x, axis, [(i, i ^ bit) for i in range(size)])


def body_small(hidden, out_grad, proj_in, proj_out, lengths, queries):
    width = proj_in.shape[0] * proj_in.shape[0]
    examples = lengths.shape[1] - 1
    per = lax.axis_size("qry")
    core, y = per, 2 * per

    def cross(x, bits):
        return swap(x, ("ex", "qry"), bits)

    q1 = swap(queries, "ex", 1)
    q2 = swap(queries, "ex", 2)
    vectors = example_vectors(hidden, out_grad, proj_in, proj_out, lengths)
    first = core + 2
    own = jnp.concatenate([vectors, cross(vectors, first)], axis=0)
    own, q2 = lax.optimization_barrier((own, q2))
    pieces = {0: own}
    for bits in (core + y, core + 1, core + y + 1):
        pieces[bits] = cross(own, bits)
    for bits in tuple(pieces):
        pieces[bits ^ core] = cross(pieces[bits], core)
    q3 = swap(q2, "ex", 1)
    rows = sorted((bits ^ (first * half), k, half) for k, bits in enumerate(pieces) for half in range(2))
    mine = per * examples
    count = queries.shape[0]
    return pl.pallas_call(
        lambda *refs: scores_kernel(*refs, width=width, rows=rows),
        out_shape=jax.ShapeDtypeStruct((mine, count), F32),
        in_specs=[pl.BlockSpec(memory_space=pltpu.VMEM)] * (len(pieces) + 4),
        out_specs=pl.BlockSpec(memory_space=pltpu.VMEM),
        compiler_params=pltpu.CompilerParams(vmem_limit_bytes=24 * 2**20),
    )(*pieces.values(), queries, q1, q2, q3)


def body_large(hidden, out_grad, proj_in, proj_out, lengths, queries):
    width = proj_in.shape[0] * proj_in.shape[0]
    vectors = example_vectors(hidden, out_grad, proj_in, proj_out, lengths)
    every = lax.all_gather(vectors, ("ex", "qry"), axis=0, tiled=True)
    total = every.shape[0]
    gram = lax.dot_general(every, every, NT, precision=HIGHEST) / total
    damp = 0.1 * jnp.trace(gram) / width + 1e-05
    factor = jnp.linalg.cholesky(gram + damp * jnp.eye(total, dtype=F32))
    mine = total // lax.axis_size("ex")
    pick = jnp.eye(total, dtype=F32)
    own = lax.dynamic_slice_in_dim(pick, lax.axis_index("ex") * mine, mine, axis=1)
    middle = lax.linalg.triangular_solve(factor, own, left_side=True, lower=True)
    solved = lax.linalg.triangular_solve(factor, middle, left_side=True, lower=True, transpose_a=True)
    weighted = lax.dot_general(solved, every, (((0,), (0,)), ((), ())), precision=HIGHEST)
    features = lax.all_gather(queries, "ex", axis=1, tiled=True).astype(F32)
    return lax.dot_general(weighted, features, NT, precision=HIGHEST)


def solution(mesh):
    placed = (
        P(("grp", "ex", "qry"), None),
        P(("grp", "ex", "qry"), None),
        P(),
        P(),
        P(("grp", "ex", "qry"), None),
        P(("grp", "qry"), "ex"),
    )
    small = mesh.shape["ex"] == 4 and mesh.shape["qry"] == 4
    return jax.shard_map(
        body_small if small else body_large,
        mesh=mesh,
        in_specs=placed,
        out_specs=P(("grp", "ex"), "qry"),
        check_vma=False,
    )
```

```python
import jax
import jax.numpy as jnp
from jax import lax
from jax.experimental import pallas as pl
from jax.experimental.pallas import tpu as pltpu
from jax.sharding import PartitionSpec as P

HIGHEST = lax.Precision.HIGHEST
F32 = jnp.float32
BF16 = jnp.bfloat16
NT = (((1,), (1,)), ((), ()))
NN = (((1,), (0,)), ((), ()))


def dot(a, b, dims=NN, precision=None):
    return lax.dot_general(a, b, dims, precision=precision, preferred_element_type=F32)


def split2(x):
    hi = x.astype(BF16)
    return hi, (x - hi.astype(F32)).astype(BF16)


def split3(x):
    hi = x.astype(BF16)
    rest = x - hi.astype(F32)
    mid = rest.astype(BF16)
    return hi, mid, (rest - mid.astype(F32)).astype(BF16)


STEPS = 4


def vectors_kernel(
    lengths, hidden, out_grad, proj_in, proj_out, vectors, tokens_in, tokens_out, rows_in, rows_out, counts, stacked, sems
):
    rank, examples = proj_in.shape[0], vectors.shape[0]
    tokens = hidden.shape[0]
    count_copy = pltpu.make_async_copy(lengths, counts, sems.at[STEPS, 0])

    def copies(step):
        pairs = ((proj_out, rows_out), (out_grad, tokens_out), (proj_in, rows_in), (hidden, tokens_in))
        made = []
        for k, (source, target) in enumerate(pairs):
            size = source.shape[1] // STEPS
            part = pl.ds(pl.multiple_of(step * size, 128), size)
            made.append(pltpu.make_async_copy(source.at[:, part], target.at[:, part], sems.at[step, k]))
        return made

    for step in range(STEPS):
        for copy in copies(step):
            copy.start()
    count_copy.start()

    def project(step, sums):
        for copy in copies(step):
            copy.wait()
        new = []
        for total, weights, x in ((sums[0], rows_out, tokens_out), (sums[1], rows_in, tokens_in)):
            size = x.shape[1] // STEPS
            part = pl.ds(pl.multiple_of(step * size, 128), size)
            new.append(total + dot(weights[:, part], x[:, part], NT))
        return tuple(new)

    nothing = jnp.zeros((rank, tokens), F32)
    side_out, side_in = lax.fori_loop(0, STEPS, project, (nothing, nothing))
    count_copy.wait()
    place = lax.broadcasted_iota(jnp.int32, (1, tokens), 1)
    rows = []
    start = jnp.int32(0)
    for e in range(examples):
        end = start + counts[0, e]
        rows.append(jnp.where((place >= start) & (place < end), side_out, 0.0))
        start = end
    stacked[:, :rank] = dot(jnp.concatenate(rows, axis=0), side_in, NT, HIGHEST)
    per = 128 // rank
    lane = lax.broadcasted_iota(jnp.int32, (examples, 128), 1) // rank
    for block in range(rank // per):
        total = None
        for k in range(per):
            piece = stacked[pl.ds(block * per + k, examples, stride=rank), :]
            if k:
                piece = jnp.where(lane == k, pltpu.roll(piece, k * rank, axis=1), total)
            total = piece
        vectors[:, block * 128:(block + 1) * 128] = total


def example_vectors(hidden, out_grad, proj_in, proj_out, lengths):
    rank, features = proj_in.shape
    width_out = proj_out.shape[1]
    tokens = hidden.shape[0]
    examples = lengths.shape[1] - 1
    operands = (lengths, hidden, out_grad, proj_in, proj_out)
    return pl.pallas_call(
        vectors_kernel,
        in_specs=[pl.BlockSpec(memory_space=pltpu.HBM)] * 5,
        out_specs=pl.BlockSpec(memory_space=pltpu.VMEM),
        out_shape=jax.ShapeDtypeStruct((examples, rank * rank), F32),
        scratch_shapes=[
            pltpu.VMEM((tokens, features), BF16),
            pltpu.VMEM((tokens, width_out), BF16),
            pltpu.VMEM((rank, features), BF16),
            pltpu.VMEM((rank, width_out), BF16),
            pltpu.SMEM(lengths.shape, jnp.int32),
            pltpu.VMEM((rank * examples, 128), F32),
            pltpu.SemaphoreType.DMA((STEPS + 1, 4)),
        ],
        compiler_params=pltpu.CompilerParams(vmem_limit_bytes=24 * 2**20),
        cost_estimate=pl.CostEstimate(
            flops=2 * tokens * rank * (features + width_out),
            bytes_accessed=2 * (tokens + rank) * (features + width_out),
            transcendentals=0,
        ),
    )(*(pltpu.with_memory_space_constraint(x, pltpu.HBM) for x in operands))


def product(a, b):
    ah, am = split2(a)
    bh, bm = split2(b)
    right = jnp.concatenate(
        [jnp.concatenate([bh, bm], axis=1), jnp.concatenate([bh, jnp.zeros_like(bm)], axis=1)], axis=0
    )
    both = dot(jnp.concatenate([ah, am], axis=1), right)
    n = b.shape[1]
    return both[:, :n] + both[:, n:]


def product6(a, b):
    ah, am, al = split3(a)
    bh, bm, bl = split3(b)
    top = jnp.concatenate([bh, bm], axis=1)
    both = dot(jnp.concatenate([ah, am], axis=1), jnp.concatenate([top, top], axis=0))
    small = dot(jnp.concatenate([al, ah], axis=1), jnp.concatenate([bh, bl], axis=0))
    n = b.shape[1]
    return both[:, :n] + (both[:, n:] + small)


def scores_kernel(*refs, width, rows):
    *pieces, q0, q1, q2, q3, out = refs
    ex, qry = lax.axis_index("ex"), lax.axis_index("qry")
    block = q0.shape[1]
    mine = out.shape[0]
    groups = lax.axis_size("qry")
    each = mine // groups
    columns = []
    for k in range(4):
        part = pl.ds(pl.multiple_of((ex ^ k) * block, block), block)
        columns.append(jnp.concatenate([pieces[p][half * each:(half + 1) * each, part] for _, p, half in rows], axis=0))
    vec = jnp.concatenate(columns, axis=1)
    n = vec.shape[0]
    vh, vm, vl = split3(vec)
    large = jnp.concatenate([vh, vm], axis=0)
    quads = dot(large, large, NT)
    tail = dot(vh, vl, NT)
    gram = quads[:n, :n] + ((quads[:n, n:] + quads[n:, :n]) + (quads[n:, n:] + (tail + tail.T)))
    gram = gram / n
    row = lax.broadcasted_iota(jnp.int32, (n, n), 0)
    col = lax.broadcasted_iota(jnp.int32, (n, n), 1)
    eye = jnp.where(row == col, 1.0, 0.0).astype(F32)
    diag_col = jnp.sum(vec * vec, axis=1, keepdims=True) / n
    diag_row = jnp.sum(eye * diag_col, axis=0, keepdims=True)
    damp = 0.1 * jnp.sum(diag_col, axis=0, keepdims=True) / width + 1e-05
    root_row = lax.rsqrt(diag_row + damp)
    root_col = lax.rsqrt(diag_col + damp)
    system = (gram + damp * eye) * root_row * root_col
    square = product(system, system)
    size = jnp.max(jnp.sum(jnp.abs(square), axis=0, keepdims=True), axis=1, keepdims=True)
    safe = (1.0 / 0.51) * lax.rsqrt(size)
    scale = (1.0 / 0.42) * lax.rsqrt(size)
    scaled = system * scale
    power = (eye - 2.0 * scaled) + square * (scale * scale)
    series = 2.0 * eye - scaled
    for _ in range(2):
        both = product(jnp.concatenate([series, power], axis=0), power)
        series = series + both[:n]
        power = both[n:]
    series = (series + product(series, power)) * scale

    wanted = jnp.concatenate([q[...] for q in (q0, q1, q2, q3)], axis=1)
    crossed = dot(jnp.concatenate([vh, vm, vl], axis=0), wanted, NT)
    cross = crossed[:n] + (crossed[n:2 * n] + crossed[2 * n:])

    def refine(x):
        error = eye - product6(system, x)
        return x + product(x, error), jnp.sum(error * error)

    def store(result):
        for away in range(groups):
            to = pl.multiple_of((qry ^ away) * each, each)
            out[pl.ds(to, each), :] = result[away * each:(away + 1) * each]

    inverse, miss = refine(series)
    store(dot(inverse[:mine] * root_row * root_col[:mine], cross, NN, HIGHEST))

    @pl.when(jnp.logical_not(miss < 1e-4))
    def _():
        def again(state):
            x, _, turns = state
            x, left = refine(x)
            return x, left, turns + 1

        begin = jnp.where(miss < 0.25, inverse, eye * safe)
        found, _, _ = lax.while_loop(
            lambda s: (s[1] > 1e-4) & (s[2] < 24), again, (begin, miss + 1.0, jnp.int32(0))
        )
        right = cross * root_col

        def correct(_, z):
            return z + dot(found, right - dot(system, z, NN, HIGHEST), NN, HIGHEST)

        solved = lax.fori_loop(0, 6, correct, jnp.zeros_like(right))
        store(solved[:mine] * root_col[:mine])


def swap(x, axis, bit):
    size = lax.axis_size(axis)
    return lax.ppermute(x, axis, [(i, i ^ bit) for i in range(size)])


def body_small(hidden, out_grad, proj_in, proj_out, lengths, queries):
    width = proj_in.shape[0] * proj_in.shape[0]
    examples = lengths.shape[1] - 1
    per = lax.axis_size("qry")
    core, y = per, 2 * per

    def cross(x, bits):
        return swap(x, ("ex", "qry"), bits)

    q1 = swap(queries, "ex", 1)
    q2 = swap(queries, "ex", 2)
    vectors = example_vectors(hidden, out_grad, proj_in, proj_out, lengths)
    first = core + 2
    own = jnp.concatenate([vectors, cross(vectors, first)], axis=0)
    own, q2 = lax.optimization_barrier((own, q2))
    pieces = {0: own}
    for bits in (core + y, core + 1, core + y + 1):
        pieces[bits] = cross(own, bits)
    for bits in tuple(pieces):
        pieces[bits ^ core] = cross(pieces[bits], core)
    q3 = swap(q2, "ex", 1)
    rows = sorted((bits ^ (first * half), k, half) for k, bits in enumerate(pieces) for half in range(2))
    mine = per * examples
    count = queries.shape[0]
    return pl.pallas_call(
        lambda *refs: scores_kernel(*refs, width=width, rows=rows),
        out_shape=jax.ShapeDtypeStruct((mine, count), F32),
        in_specs=[pl.BlockSpec(memory_space=pltpu.VMEM)] * (len(pieces) + 4),
        out_specs=pl.BlockSpec(memory_space=pltpu.VMEM),
        compiler_params=pltpu.CompilerParams(vmem_limit_bytes=24 * 2**20),
    )(*pieces.values(), queries, q1, q2, q3)


def body_large(hidden, out_grad, proj_in, proj_out, lengths, queries):
    width = proj_in.shape[0] * proj_in.shape[0]
    vectors = example_vectors(hidden, out_grad, proj_in, proj_out, lengths)
    every = lax.all_gather(vectors, ("ex", "qry"), axis=0, tiled=True)
    total = every.shape[0]
    gram = lax.dot_general(every, every, NT, precision=HIGHEST) / total
    damp = 0.1 * jnp.trace(gram) / width + 1e-05
    factor = jnp.linalg.cholesky(gram + damp * jnp.eye(total, dtype=F32))
    mine = total // lax.axis_size("ex")
    pick = jnp.eye(total, dtype=F32)
    own = lax.dynamic_slice_in_dim(pick, lax.axis_index("ex") * mine, mine, axis=1)
    middle = lax.linalg.triangular_solve(factor, own, left_side=True, lower=True)
    solved = lax.linalg.triangular_solve(factor, middle, left_side=True, lower=True, transpose_a=True)
    weighted = lax.dot_general(solved, every, (((0,), (0,)), ((), ())), precision=HIGHEST)
    features = lax.all_gather(queries, "ex", axis=1, tiled=True).astype(F32)
    return lax.dot_general(weighted, features, NT, precision=HIGHEST)


def solution(mesh):
    placed = (
        P(("grp", "ex", "qry"), None),
        P(("grp", "ex", "qry"), None),
        P(),
        P(),
        P(("grp", "ex", "qry"), None),
        P(("grp", "qry"), "ex"),
    )
    small = mesh.shape["ex"] == 4 and mesh.shape["qry"] == 4
    return jax.shard_map(
        body_small if small else body_large,
        mesh=mesh,
        in_specs=placed,
        out_specs=P(("grp", "ex"), "qry"),
        check_vma=False,
    )
```

```python
import jax
import jax.numpy as jnp
from jax import lax
from jax.experimental import pallas as pl
from jax.experimental.pallas import tpu as pltpu
from jax.sharding import PartitionSpec as P

HIGHEST = lax.Precision.HIGHEST
F32 = jnp.float32
BF16 = jnp.bfloat16
NT = (((1,), (1,)), ((), ()))
NN = (((1,), (0,)), ((), ()))


def dot(a, b, dims=NN, precision=None):
    return lax.dot_general(a, b, dims, precision=precision, preferred_element_type=F32)


def split2(x):
    hi = x.astype(BF16)
    return hi, (x - hi.astype(F32)).astype(BF16)


def split3(x):
    hi = x.astype(BF16)
    rest = x - hi.astype(F32)
    mid = rest.astype(BF16)
    return hi, mid, (rest - mid.astype(F32)).astype(BF16)


STEPS = 4


def vectors_kernel(
    lengths, hidden, out_grad, proj_in, proj_out, vectors, tokens_in, tokens_out, rows_in, rows_out, counts, stacked, sems
):
    rank, examples = proj_in.shape[0], vectors.shape[0]
    tokens = hidden.shape[0]
    count_copy = pltpu.make_async_copy(lengths, counts, sems.at[STEPS, 0])

    def copies(step):
        pairs = ((proj_out, rows_out), (out_grad, tokens_out), (proj_in, rows_in), (hidden, tokens_in))
        made = []
        for k, (source, target) in enumerate(pairs):
            size = source.shape[1] // STEPS
            part = pl.ds(pl.multiple_of(step * size, 128), size)
            made.append(pltpu.make_async_copy(source.at[:, part], target.at[:, part], sems.at[step, k]))
        return made

    for step in range(STEPS):
        for copy in copies(step):
            copy.start()
    count_copy.start()

    def project(step, sums):
        for copy in copies(step):
            copy.wait()
        new = []
        for total, weights, x in ((sums[0], rows_out, tokens_out), (sums[1], rows_in, tokens_in)):
            size = x.shape[1] // STEPS
            part = pl.ds(pl.multiple_of(step * size, 128), size)
            new.append(total + dot(weights[:, part], x[:, part], NT))
        return tuple(new)

    nothing = jnp.zeros((rank, tokens), F32)
    side_out, side_in = lax.fori_loop(0, STEPS, project, (nothing, nothing))
    count_copy.wait()
    place = lax.broadcasted_iota(jnp.int32, (1, tokens), 1)
    rows = []
    start = jnp.int32(0)
    for e in range(examples):
        end = start + counts[0, e]
        rows.append(jnp.where((place >= start) & (place < end), side_out, 0.0))
        start = end
    stacked[:, :rank] = dot(jnp.concatenate(rows, axis=0), side_in, NT, HIGHEST)
    per = 128 // rank
    lane = lax.broadcasted_iota(jnp.int32, (examples, 128), 1) // rank
    for block in range(rank // per):
        total = None
        for k in range(per):
            piece = stacked[pl.ds(block * per + k, examples, stride=rank), :]
            if k:
                piece = jnp.where(lane == k, pltpu.roll(piece, k * rank, axis=1), total)
            total = piece
        vectors[:, block * 128:(block + 1) * 128] = total


def example_vectors(hidden, out_grad, proj_in, proj_out, lengths):
    rank, features = proj_in.shape
    width_out = proj_out.shape[1]
    tokens = hidden.shape[0]
    examples = lengths.shape[1] - 1
    operands = (lengths, hidden, out_grad, proj_in, proj_out)
    return pl.pallas_call(
        vectors_kernel,
        in_specs=[pl.BlockSpec(memory_space=pltpu.HBM)] * 5,
        out_specs=pl.BlockSpec(memory_space=pltpu.VMEM),
        out_shape=jax.ShapeDtypeStruct((examples, rank * rank), F32),
        scratch_shapes=[
            pltpu.VMEM((tokens, features), BF16),
            pltpu.VMEM((tokens, width_out), BF16),
            pltpu.VMEM((rank, features), BF16),
            pltpu.VMEM((rank, width_out), BF16),
            pltpu.SMEM(lengths.shape, jnp.int32),
            pltpu.VMEM((rank * examples, 128), F32),
            pltpu.SemaphoreType.DMA((STEPS + 1, 4)),
        ],
        compiler_params=pltpu.CompilerParams(vmem_limit_bytes=24 * 2**20),
        cost_estimate=pl.CostEstimate(
            flops=2 * tokens * rank * (features + width_out),
            bytes_accessed=2 * (tokens + rank) * (features + width_out),
            transcendentals=0,
        ),
    )(*(pltpu.with_memory_space_constraint(x, pltpu.HBM) for x in operands))


def product(a, b):
    ah, am = split2(a)
    bh, bm = split2(b)
    right = jnp.concatenate(
        [jnp.concatenate([bh, bm], axis=1), jnp.concatenate([bh, jnp.zeros_like(bm)], axis=1)], axis=0
    )
    both = dot(jnp.concatenate([ah, am], axis=1), right)
    n = b.shape[1]
    return both[:, :n] + both[:, n:]


def product6(a, b):
    ah, am, al = split3(a)
    bh, bm, bl = split3(b)
    top = jnp.concatenate([bh, bm], axis=1)
    both = dot(jnp.concatenate([ah, am], axis=1), jnp.concatenate([top, top], axis=0))
    small = dot(jnp.concatenate([al, ah], axis=1), jnp.concatenate([bh, bl], axis=0))
    n = b.shape[1]
    return both[:, :n] + (both[:, n:] + small)


def scores_kernel(*refs, width, rows):
    *pieces, q0, q1, q2, q3, out = refs
    ex, qry = lax.axis_index("ex"), lax.axis_index("qry")
    block = q0.shape[1]
    mine = out.shape[0]
    groups = lax.axis_size("qry")
    each = mine // groups
    columns = []
    for k in range(4):
        part = pl.ds(pl.multiple_of((ex ^ k) * block, block), block)
        columns.append(jnp.concatenate([pieces[p][half * each:(half + 1) * each, part] for _, p, half in rows], axis=0))
    vec = jnp.concatenate(columns, axis=1)
    n = vec.shape[0]
    vh, vm, vl = split3(vec)
    large = jnp.concatenate([vh, vm], axis=0)
    quads = dot(large, large, NT)
    tail = dot(vh, vl, NT)
    gram = quads[:n, :n] + ((quads[:n, n:] + quads[n:, :n]) + (quads[n:, n:] + (tail + tail.T)))
    gram = gram / n
    row = lax.broadcasted_iota(jnp.int32, (n, n), 0)
    col = lax.broadcasted_iota(jnp.int32, (n, n), 1)
    eye = jnp.where(row == col, 1.0, 0.0).astype(F32)
    diag_col = jnp.sum(vec * vec, axis=1, keepdims=True) / n
    diag_row = jnp.sum(eye * diag_col, axis=0, keepdims=True)
    damp = 0.1 * jnp.sum(diag_col, axis=0, keepdims=True) / width + 1e-05
    root_row = lax.rsqrt(diag_row + damp)
    root_col = lax.rsqrt(diag_col + damp)
    system = (gram + damp * eye) * root_row * root_col
    square = product(system, system)
    size = jnp.max(jnp.sum(jnp.abs(square), axis=0, keepdims=True), axis=1, keepdims=True)
    safe = (1.0 / 0.51) * lax.rsqrt(size)
    scale = (1.0 / 0.42) * lax.rsqrt(size)
    scaled = system * scale
    power = (eye - 2.0 * scaled) + square * (scale * scale)
    series = 2.0 * eye - scaled
    for _ in range(2):
        both = product(jnp.concatenate([series, power], axis=0), power)
        series = series + both[:n]
        power = both[n:]
    series = (series + product(series, power)) * scale

    wanted = jnp.concatenate([q[...] for q in (q0, q1, q2, q3)], axis=1)
    crossed = dot(jnp.concatenate([vh, vm, vl], axis=0), wanted, NT)
    cross = crossed[:n] + (crossed[n:2 * n] + crossed[2 * n:])

    def refine(x):
        error = eye - product6(system, x)
        return x + product(x, error), jnp.sum(error * error)

    def store(result):
        for away in range(groups):
            to = pl.multiple_of((qry ^ away) * each, each)
            out[pl.ds(to, each), :] = result[away * each:(away + 1) * each]

    inverse, miss = refine(series)
    store(dot(inverse[:mine] * root_row * root_col[:mine], cross, NN, HIGHEST))

    @pl.when(jnp.logical_not(miss < 1e-4))
    def _():
        def again(state):
            x, _, turns = state
            x, left = refine(x)
            return x, left, turns + 1

        begin = jnp.where(miss < 0.25, inverse, eye * safe)
        found, _, _ = lax.while_loop(
            lambda s: (s[1] > 1e-4) & (s[2] < 24), again, (begin, miss + 1.0, jnp.int32(0))
        )
        right = cross * root_col

        def correct(_, z):
            return z + dot(found, right - dot(system, z, NN, HIGHEST), NN, HIGHEST)

        solved = lax.fori_loop(0, 6, correct, jnp.zeros_like(right))
        store(solved[:mine] * root_col[:mine])


def swap(x, axis, bit):
    size = lax.axis_size(axis)
    return lax.ppermute(x, axis, [(i, i ^ bit) for i in range(size)])


def body_small(hidden, out_grad, proj_in, proj_out, lengths, queries):
    width = proj_in.shape[0] * proj_in.shape[0]
    examples = lengths.shape[1] - 1
    per = lax.axis_size("qry")
    core, y = per, 2 * per

    def cross(x, bits):
        return swap(x, ("ex", "qry"), bits)

    q1 = swap(queries, "ex", 1)
    q2 = cross(queries, core + y)
    vectors = example_vectors(hidden, out_grad, proj_in, proj_out, lengths)
    first = core + 2
    own = jnp.concatenate([vectors, cross(vectors, first)], axis=0)
    own, q2 = lax.optimization_barrier((own, q2))
    pieces = {0: own}
    for bits in (core + y, core + 1, core + y + 1):
        pieces[bits] = cross(own, bits)
    for bits in tuple(pieces):
        pieces[bits ^ core] = cross(pieces[bits], core)
    q3 = swap(q2, "ex", 1)
    rows = sorted((bits ^ (first * half), k, half) for k, bits in enumerate(pieces) for half in range(2))
    mine = per * examples
    count = queries.shape[0]
    return pl.pallas_call(
        lambda *refs: scores_kernel(*refs, width=width, rows=rows),
        out_shape=jax.ShapeDtypeStruct((mine, count), F32),
        in_specs=[pl.BlockSpec(memory_space=pltpu.VMEM)] * (len(pieces) + 4),
        out_specs=pl.BlockSpec(memory_space=pltpu.VMEM),
        compiler_params=pltpu.CompilerParams(vmem_limit_bytes=24 * 2**20),
    )(*pieces.values(), queries, q1, q3, q2)


def body_large(hidden, out_grad, proj_in, proj_out, lengths, queries):
    width = proj_in.shape[0] * proj_in.shape[0]
    vectors = example_vectors(hidden, out_grad, proj_in, proj_out, lengths)
    every = lax.all_gather(vectors, ("ex", "qry"), axis=0, tiled=True)
    total = every.shape[0]
    gram = lax.dot_general(every, every, NT, precision=HIGHEST) / total
    damp = 0.1 * jnp.trace(gram) / width + 1e-05
    factor = jnp.linalg.cholesky(gram + damp * jnp.eye(total, dtype=F32))
    mine = total // lax.axis_size("ex")
    pick = jnp.eye(total, dtype=F32)
    own = lax.dynamic_slice_in_dim(pick, lax.axis_index("ex") * mine, mine, axis=1)
    middle = lax.linalg.triangular_solve(factor, own, left_side=True, lower=True)
    solved = lax.linalg.triangular_solve(factor, middle, left_side=True, lower=True, transpose_a=True)
    weighted = lax.dot_general(solved, every, (((0,), (0,)), ((), ())), precision=HIGHEST)
    features = lax.all_gather(queries, "ex", axis=1, tiled=True).astype(F32)
    return lax.dot_general(weighted, features, NT, precision=HIGHEST)


def solution(mesh):
    placed = (
        P(("grp", "ex", "qry"), None),
        P(("grp", "ex", "qry"), None),
        P(),
        P(),
        P(("grp", "ex", "qry"), None),
        P(("grp", "qry"), "ex"),
    )
    small = mesh.shape["ex"] == 4 and mesh.shape["qry"] == 4
    return jax.shard_map(
        body_small if small else body_large,
        mesh=mesh,
        in_specs=placed,
        out_specs=P(("grp", "ex"), "qry"),
        check_vma=False,
    )
```

```python
import jax
import jax.numpy as jnp
from jax import lax
from jax.experimental import pallas as pl
from jax.experimental.pallas import tpu as pltpu
from jax.sharding import PartitionSpec as P

HIGHEST = lax.Precision.HIGHEST
F32 = jnp.float32
BF16 = jnp.bfloat16
NT = (((1,), (1,)), ((), ()))
NN = (((1,), (0,)), ((), ()))


def dot(a, b, dims=NN, precision=None):
    return lax.dot_general(a, b, dims, precision=precision, preferred_element_type=F32)


def split2(x):
    hi = x.astype(BF16)
    return hi, (x - hi.astype(F32)).astype(BF16)


def split3(x):
    hi = x.astype(BF16)
    rest = x - hi.astype(F32)
    mid = rest.astype(BF16)
    return hi, mid, (rest - mid.astype(F32)).astype(BF16)


STEPS = 4


def vectors_kernel(
    lengths, hidden, out_grad, proj_in, proj_out, vectors, tokens_in, tokens_out, rows_in, rows_out, counts, stacked, sems
):
    rank, examples = proj_in.shape[0], vectors.shape[0]
    tokens = hidden.shape[0]
    count_copy = pltpu.make_async_copy(lengths, counts, sems.at[STEPS, 0])

    def copies(step):
        pairs = ((proj_out, rows_out), (out_grad, tokens_out), (proj_in, rows_in), (hidden, tokens_in))
        made = []
        for k, (source, target) in enumerate(pairs):
            size = source.shape[1] // STEPS
            part = pl.ds(pl.multiple_of(step * size, 128), size)
            made.append(pltpu.make_async_copy(source.at[:, part], target.at[:, part], sems.at[step, k]))
        return made

    for step in range(STEPS):
        for copy in copies(step):
            copy.start()
    count_copy.start()

    def project(step, sums):
        for copy in copies(step):
            copy.wait()
        new = []
        for total, weights, x in ((sums[0], rows_out, tokens_out), (sums[1], rows_in, tokens_in)):
            size = x.shape[1] // STEPS
            part = pl.ds(pl.multiple_of(step * size, 128), size)
            new.append(total + dot(weights[:, part], x[:, part], NT))
        return tuple(new)

    nothing = jnp.zeros((rank, tokens), F32)
    side_out, side_in = lax.fori_loop(0, STEPS, project, (nothing, nothing))
    count_copy.wait()
    place = lax.broadcasted_iota(jnp.int32, (1, tokens), 1)
    rows = []
    start = jnp.int32(0)
    for e in range(examples):
        end = start + counts[0, e]
        rows.append(jnp.where((place >= start) & (place < end), side_out, 0.0))
        start = end
    stacked[:, :rank] = dot(jnp.concatenate(rows, axis=0), side_in, NT, HIGHEST)
    per = 128 // rank
    lane = lax.broadcasted_iota(jnp.int32, (examples, 128), 1) // rank
    for block in range(rank // per):
        total = None
        for k in range(per):
            piece = stacked[pl.ds(block * per + k, examples, stride=rank), :]
            if k:
                piece = jnp.where(lane == k, pltpu.roll(piece, k * rank, axis=1), total)
            total = piece
        vectors[:, block * 128:(block + 1) * 128] = total


def example_vectors(hidden, out_grad, proj_in, proj_out, lengths):
    rank, features = proj_in.shape
    width_out = proj_out.shape[1]
    tokens = hidden.shape[0]
    examples = lengths.shape[1] - 1
    operands = (lengths, hidden, out_grad, proj_in, proj_out)
    return pl.pallas_call(
        vectors_kernel,
        in_specs=[pl.BlockSpec(memory_space=pltpu.HBM)] * 5,
        out_specs=pl.BlockSpec(memory_space=pltpu.VMEM),
        out_shape=jax.ShapeDtypeStruct((examples, rank * rank), F32),
        scratch_shapes=[
            pltpu.VMEM((tokens, features), BF16),
            pltpu.VMEM((tokens, width_out), BF16),
            pltpu.VMEM((rank, features), BF16),
            pltpu.VMEM((rank, width_out), BF16),
            pltpu.SMEM(lengths.shape, jnp.int32),
            pltpu.VMEM((rank * examples, 128), F32),
            pltpu.SemaphoreType.DMA((STEPS + 1, 4)),
        ],
        compiler_params=pltpu.CompilerParams(vmem_limit_bytes=24 * 2**20),
        cost_estimate=pl.CostEstimate(
            flops=2 * tokens * rank * (features + width_out),
            bytes_accessed=2 * (tokens + rank) * (features + width_out),
            transcendentals=0,
        ),
    )(*(pltpu.with_memory_space_constraint(x, pltpu.HBM) for x in operands))


def product(a, b):
    ah, am = split2(a)
    bh, bm = split2(b)
    right = jnp.concatenate(
        [jnp.concatenate([bh, bm], axis=1), jnp.concatenate([bh, jnp.zeros_like(bm)], axis=1)], axis=0
    )
    both = dot(jnp.concatenate([ah, am], axis=1), right)
    n = b.shape[1]
    return both[:, :n] + both[:, n:]


def product6(a, b):
    ah, am, al = split3(a)
    bh, bm, bl = split3(b)
    top = jnp.concatenate([bh, bm], axis=1)
    both = dot(jnp.concatenate([ah, am], axis=1), jnp.concatenate([top, top], axis=0))
    small = dot(jnp.concatenate([al, ah], axis=1), jnp.concatenate([bh, bl], axis=0))
    n = b.shape[1]
    return both[:, :n] + (both[:, n:] + small)


def scores_kernel(*refs, width, rows):
    *pieces, q0, q1, q2, q3, out = refs
    ex, qry = lax.axis_index("ex"), lax.axis_index("qry")
    block = q0.shape[1]
    mine = out.shape[0]
    groups = lax.axis_size("qry")
    each = mine // groups
    columns = []
    for k in range(4):
        part = pl.ds(pl.multiple_of((ex ^ k) * block, block), block)
        columns.append(jnp.concatenate([pieces[p][half * each:(half + 1) * each, part] for _, p, half in rows], axis=0))
    vec = jnp.concatenate(columns, axis=1)
    n = vec.shape[0]
    vh, vm, vl = split3(vec)
    large = jnp.concatenate([vh, vm], axis=0)
    quads = dot(large, large, NT)
    tail = dot(vh, vl, NT)
    gram = quads[:n, :n] + ((quads[:n, n:] + quads[n:, :n]) + (quads[n:, n:] + (tail + tail.T)))
    gram = gram / n
    row = lax.broadcasted_iota(jnp.int32, (n, n), 0)
    col = lax.broadcasted_iota(jnp.int32, (n, n), 1)
    eye = jnp.where(row == col, 1.0, 0.0).astype(F32)
    diag_col = jnp.sum(vec * vec, axis=1, keepdims=True) / n
    diag_row = jnp.sum(eye * diag_col, axis=0, keepdims=True)
    damp = 0.1 * jnp.sum(diag_col, axis=0, keepdims=True) / width + 1e-05
    root_row = lax.rsqrt(diag_row + damp)
    root_col = lax.rsqrt(diag_col + damp)
    system = (gram + damp * eye) * root_row * root_col
    square = product(system, system)
    size = jnp.max(jnp.sum(jnp.abs(square), axis=0, keepdims=True), axis=1, keepdims=True)
    safe = (1.0 / 0.51) * lax.rsqrt(size)
    scale = (1.0 / 0.42) * lax.rsqrt(size)
    scaled = system * scale
    power = (eye - 2.0 * scaled) + square * (scale * scale)
    series = 2.0 * eye - scaled
    for _ in range(2):
        both = product(jnp.concatenate([series, power], axis=0), power)
        series = series + both[:n]
        power = both[n:]
    series = (series + product(series, power)) * scale

    wanted = jnp.concatenate([q[...] for q in (q0, q1, q2, q3)], axis=1)
    crossed = dot(jnp.concatenate([vh, vm, vl], axis=0), wanted, NT)
    cross = crossed[:n] + (crossed[n:2 * n] + crossed[2 * n:])

    def refine(x):
        error = eye - product6(system, x)
        return x + product(x, error), jnp.sum(error * error)

    def store(result):
        for away in range(groups):
            to = pl.multiple_of((qry ^ away) * each, each)
            out[pl.ds(to, each), :] = result[away * each:(away + 1) * each]

    inverse, miss = refine(series)
    store(dot(inverse[:mine] * root_row * root_col[:mine], cross, NN, HIGHEST))

    @pl.when(jnp.logical_not(miss < 1e-4))
    def _():
        def again(state):
            x, _, turns = state
            x, left = refine(x)
            return x, left, turns + 1

        begin = jnp.where(miss < 0.25, inverse, eye * safe)
        found, _, _ = lax.while_loop(
            lambda s: (s[1] > 1e-4) & (s[2] < 24), again, (begin, miss + 1.0, jnp.int32(0))
        )
        right = cross * root_col

        def correct(_, z):
            return z + dot(found, right - dot(system, z, NN, HIGHEST), NN, HIGHEST)

        solved = lax.fori_loop(0, 6, correct, jnp.zeros_like(right))
        store(solved[:mine] * root_col[:mine])


def swap(x, axis, bit):
    size = lax.axis_size(axis)
    return lax.ppermute(x, axis, [(i, i ^ bit) for i in range(size)])


def body_small(hidden, out_grad, proj_in, proj_out, lengths, queries):
    width = proj_in.shape[0] * proj_in.shape[0]
    examples = lengths.shape[1] - 1
    per = lax.axis_size("qry")
    core, y = per, 2 * per

    def cross(x, bits):
        return swap(x, ("ex", "qry"), bits)

    q1 = swap(queries, "ex", 1)
    q2 = cross(queries, core + y)
    vectors = example_vectors(hidden, out_grad, proj_in, proj_out, lengths)
    first = core + 2
    own = jnp.concatenate([vectors, cross(vectors, first)], axis=0)
    own, q2 = lax.optimization_barrier((own, q2))
    pieces = {0: own}
    for bits in (core + y, 1, core + y + 1):
        pieces[bits] = cross(own, bits)
    for bits in tuple(pieces):
        pieces[bits ^ core] = cross(pieces[bits], core)
    q3 = swap(q2, "ex", 1)
    rows = sorted((bits ^ (first * half), k, half) for k, bits in enumerate(pieces) for half in range(2))
    mine = per * examples
    count = queries.shape[0]
    return pl.pallas_call(
        lambda *refs: scores_kernel(*refs, width=width, rows=rows),
        out_shape=jax.ShapeDtypeStruct((mine, count), F32),
        in_specs=[pl.BlockSpec(memory_space=pltpu.VMEM)] * (len(pieces) + 4),
        out_specs=pl.BlockSpec(memory_space=pltpu.VMEM),
        compiler_params=pltpu.CompilerParams(vmem_limit_bytes=24 * 2**20),
    )(*pieces.values(), queries, q1, q3, q2)


def body_large(hidden, out_grad, proj_in, proj_out, lengths, queries):
    width = proj_in.shape[0] * proj_in.shape[0]
    vectors = example_vectors(hidden, out_grad, proj_in, proj_out, lengths)
    every = lax.all_gather(vectors, ("ex", "qry"), axis=0, tiled=True)
    total = every.shape[0]
    gram = lax.dot_general(every, every, NT, precision=HIGHEST) / total
    damp = 0.1 * jnp.trace(gram) / width + 1e-05
    factor = jnp.linalg.cholesky(gram + damp * jnp.eye(total, dtype=F32))
    mine = total // lax.axis_size("ex")
    pick = jnp.eye(total, dtype=F32)
    own = lax.dynamic_slice_in_dim(pick, lax.axis_index("ex") * mine, mine, axis=1)
    middle = lax.linalg.triangular_solve(factor, own, left_side=True, lower=True)
    solved = lax.linalg.triangular_solve(factor, middle, left_side=True, lower=True, transpose_a=True)
    weighted = lax.dot_general(solved, every, (((0,), (0,)), ((), ())), precision=HIGHEST)
    features = lax.all_gather(queries, "ex", axis=1, tiled=True).astype(F32)
    return lax.dot_general(weighted, features, NT, precision=HIGHEST)


def solution(mesh):
    placed = (
        P(("grp", "ex", "qry"), None),
        P(("grp", "ex", "qry"), None),
        P(),
        P(),
        P(("grp", "ex", "qry"), None),
        P(("grp", "qry"), "ex"),
    )
    small = mesh.shape["ex"] == 4 and mesh.shape["qry"] == 4
    return jax.shard_map(
        body_small if small else body_large,
        mesh=mesh,
        in_specs=placed,
        out_specs=P(("grp", "ex"), "qry"),
        check_vma=False,
    )
```
